512 devices in a mesh: ctx: 16 (over y, core), enc: 32 (over z, x).
Axes of the slice: x: 4, y: 8, z: 8, core: 2. Of those that a mesh axis runs over, the one named last changes fastest.
Arguments:
- queries: bfloat16 [32, 2048, 4096], P('enc', 'ctx'), may hold values from -200 to 200
- d_out: bfloat16 [32, 2048, 4096], P('enc', 'ctx'), may hold values from -24 to 24
- text_sample: int32 [32, 2048], P('enc', 'ctx'), may hold values from 0 to 1, as said below
- tiles: int32 [32, 2], P('enc'), may hold values from 1 to 4
- img_k: bfloat16 [32, 512, 1024], P(None, ('ctx', 'enc')), may hold values from -20 to 20
- img_v: bfloat16 [32, 512, 1024], P(None, ('ctx', 'enc')), may hold values from -6 to 6
Outputs:
- d_queries: bfloat16 [32, 2048, 4096], P('enc', 'ctx')
- d_img_k: bfloat16 [32, 512, 1024], P(None, ('ctx', 'enc'))
- d_img_v: bfloat16 [32, 512, 1024], P(None, ('ctx', 'enc'))
The draws below stay inside these ranges and needn't reach their ends.
Inputs may be any that keep to these rules, and one draw needn't show every extreme that they name: `text_sample`: within each group the sample numbers never fall along the text, and each of the 2 samples has at least one token.
All inputs are finite; a program needn't handle non-finite values.
Results may differ from the reference program's by a relative error of at most 0.022.
Values may be sent and summed in bfloat16 or wider, within the bound.
A program may use at most 128 MiB of HBM per device.

```python
import jax
import jax.numpy as jnp
from jax import lax

H = 32
KVH = 8
HD = 128
SAMP = 2
MAX_TILES = 4
TILE_TOK = 64
TEXT_GRP = 2048
KEYS_GRP = 512
N_ENC = 32


def shared_draw(key):
    sample_key = jax.random.fold_in(key, 101)
    base_key = jax.random.fold_in(key, 102)
    group_keys = jax.random.split(sample_key, N_ENC)
    cuts = jax.vmap(lambda one_key: jax.random.permutation(one_key, TEXT_GRP - 1)[:SAMP - 1] + 1)(group_keys)
    positions = jnp.arange(TEXT_GRP, dtype=jnp.int32)
    samples = jnp.sum((positions[None, :, None] >= cuts[:, None, :]).astype(jnp.int32), axis=-1).astype(jnp.int32)
    base = jax.random.truncated_normal(base_key, -6.0, 6.0, (N_ENC, KEYS_GRP, KVH * HD), jnp.float32)
    return (samples, base)


def draw_text_sample(key, part):
    samples, base = shared_draw(key)
    return samples


def draw_img_k(key, part):
    samples, base = shared_draw(key)
    result = base
    return result.astype(jnp.bfloat16)


def draw_queries(key, part):
    key = jax.random.fold_in(key, 9)
    normal_key = jax.random.fold_in(key, 0)
    values = jax.random.truncated_normal(normal_key, -6.0, 6.0, (N_ENC, TEXT_GRP, H, HD), jnp.float32)
    return values.reshape(N_ENC, TEXT_GRP, H * HD).astype(jnp.bfloat16)


def place_ends(array, own_key, smallest, high):
    spot = [jax.random.randint(jax.random.fold_in(own_key, axis), (), 0, length) for axis, length in enumerate(array.shape)]
    longest = array.shape.index(max(array.shape))
    beside = spot[:longest] + [(spot[longest] + 1) % array.shape[longest]] + spot[longest + 1:]
    return array.at[tuple(spot)].set(smallest).at[tuple(beside)].set(high)


def block_levels(own_key, extent, pieces, low, largest):
    def one(position, parts):
        heights = jax.random.uniform(jax.random.fold_in(jax.random.fold_in(own_key, 6), position), (parts,), jnp.float32, low / len(pieces), largest / len(pieces))
        return jnp.repeat(jnp.exp(heights), extent[position] // parts).reshape((-1,) + (1,) * (len(extent) - position - 1))

    level = one(*pieces[0])
    for cut in pieces[1:]:
        level = level * one(*cut)
    return level


def bell_draw(rng, dims, width, bound, pieces=(), held_as=jnp.bfloat16):
    gain = block_levels(rng, dims, pieces, -0.22, 0.18) if pieces else 1.0
    drawn = jax.random.normal(rng, dims, jnp.float32) * width * gain
    return jnp.minimum(jnp.maximum(drawn, -bound), bound).astype(held_as)


def setup_inputs(seed: int = 0) -> dict:
    key_of = jax.random.split(jax.random.key(seed), 7)
    queries = draw_queries(jax.random.fold_in(key_of[6], 71), 0)
    d_out = bell_draw(key_of[1], (N_ENC, TEXT_GRP, H * HD), 4.0, 24.0, ((0, 32), (1, 16)))
    text_sample = draw_text_sample(jax.random.fold_in(key_of[6], 71), 0)
    tiles = place_ends(jax.random.randint(key_of[3], (N_ENC, SAMP), 1, MAX_TILES + 1), jax.random.fold_in(key_of[3], 1), 1, MAX_TILES).astype(jnp.int32)
    img_k = draw_img_k(jax.random.fold_in(key_of[6], 71), 0)
    img_v = bell_draw(key_of[5], (N_ENC, KEYS_GRP, KVH * HD), 1.0, 6.0, ((1, 512),))
    return dict(queries=queries, d_out=d_out, text_sample=text_sample, tiles=tiles, img_k=img_k, img_v=img_v)


big_negative = -1e30


def reference(queries, d_out, text_sample, tiles, img_k, img_v):
    group_ratio = H // KVH
    score_scale = HD ** -0.5
    slot_rows = MAX_TILES * TILE_TOK

    def one_group(items):
        query_rows, grad_rows, sample_rows, tile_row, key_rows, value_rows = items
        token_count = query_rows.shape[0]
        query_heads = query_rows.astype(jnp.float32).reshape(token_count, KVH, group_ratio, HD)
        grad_heads = grad_rows.astype(jnp.float32).reshape(token_count, KVH, group_ratio, HD)
        key_heads = key_rows.astype(jnp.float32).reshape(KEYS_GRP, KVH, HD)
        value_heads = value_rows.astype(jnp.float32).reshape(KEYS_GRP, KVH, HD)
        key_index = jnp.arange(KEYS_GRP, dtype=jnp.int32)
        key_sample = key_index // slot_rows
        key_tile = (key_index % slot_rows) // TILE_TOK
        valid = key_tile < tile_row[key_sample]
        allowed = (sample_rows[:, None] == key_sample[None, :]) & valid[None, :]
        scores = jnp.einsum("tagd,kad->agtk", query_heads, key_heads) * score_scale
        scores = jnp.where(allowed, scores, big_negative)
        row_max = jnp.max(scores, axis=-1)
        weights = jnp.where(allowed, jnp.exp(scores - row_max[..., None]), 0.0)
        log_total = row_max + jnp.log(jnp.sum(weights, axis=-1))
        probs = jnp.where(allowed, jnp.exp(scores - log_total[..., None]), 0.0)
        grad_probs = jnp.einsum("tagd,kad->agtk", grad_heads, value_heads)
        row_dot = jnp.sum(probs * grad_probs, axis=-1)
        grad_scores = (probs * (grad_probs - row_dot[..., None]) * score_scale).astype(jnp.bfloat16)
        probs_half = probs.astype(jnp.bfloat16)
        grad_query = jnp.einsum("agtk,kad->tagd", grad_scores.astype(jnp.float32), key_heads)
        grad_key = jnp.einsum("agtk,tagd->kad", grad_scores.astype(jnp.float32), query_heads)
        grad_value = jnp.einsum("agtk,tagd->kad", probs_half.astype(jnp.float32), grad_heads)
        return (grad_query.reshape(token_count, H * HD).astype(jnp.bfloat16),
                grad_key.reshape(KEYS_GRP, KVH * HD).astype(jnp.bfloat16),
                grad_value.reshape(KEYS_GRP, KVH * HD).astype(jnp.bfloat16))

    d_queries, d_img_k, d_img_v = lax.map(one_group, (queries, d_out, text_sample, tiles, img_k, img_v))
    return (d_queries, d_img_k, d_img_v)
```

```python
import functools
import math

import jax
import jax.numpy as jnp
from jax import lax
from jax.experimental import pallas as pl
from jax.experimental.pallas import tpu as pltpu
from jax.sharding import PartitionSpec as P

H = 32
KVH = 8
HD = 128
SAMP = 2
MAX_TILES = 4
RING = SAMP * MAX_TILES
HALF_KV = KVH // 2
RATIO = H // KVH
SCALE = HD ** -0.5
EXP2_SCALE = SCALE * math.log2(math.e)

big_negative = -1e30

MESH = pl.DeviceIdType.MESH
F32 = jnp.float32
BF16 = jnp.bfloat16


def remote(src, dst, send_sem, recv_sem, ctx, enc):
    return pltpu.make_async_remote_copy(
        src_ref=src,
        dst_ref=dst,
        send_sem=send_sem,
        recv_sem=recv_sem,
        device_id=(ctx, enc),
        device_id_type=MESH,
    )


def nt_dot(a, b):
    return lax.dot_general(a, b, (((1,), (1,)), ((), ())), preferred_element_type=F32)


def kernel(
    n_enc,
    tiles_ref,
    text_ref,
    own_ref,
    q_ref,
    do_ref,
    dq_ref,
    dkv_ref,
    text_buf,
    late_mask,
    q_buf,
    do_buf,
    dq_buf,
    slots,
    rows,
    kv,
    ds_all,
    p_all,
    qc_all,
    dc_all,
    part,
    rs_send,
    rs_recv,
    load_sem,
    swap_send,
    swap_recv,
    in_send,
    in_recv,
    ag_send,
    ag_recv,
    red_send,
    red_recv,
    out_send,
    out_recv,
    dq_sem,
    dq_send,
    dq_recv,
):
    ctx = lax.axis_index("ctx")
    enc = lax.axis_index("enc")
    y = ctx // 2
    core = lax.rem(ctx, 2)
    other = 1 - core
    twin = 2 * y + other
    right = 2 * lax.rem(y + 1, RING) + core
    left = 2 * lax.rem(y + RING - 1, RING) + core
    tokens = q_ref.shape[0]
    width = q_ref.shape[1] // 2
    tile = 2 * n_enc
    span = MAX_TILES * tile

    mine = pl.ds(pl.multiple_of(core * width, width), width)
    theirs = pl.ds(pl.multiple_of(other * width, width), width)

    load_q = pltpu.make_async_copy(q_ref.at[:, mine], q_buf.at[core], load_sem.at[0])
    load_do = pltpu.make_async_copy(do_ref.at[:, mine], do_buf.at[core], load_sem.at[1])
    load_q.start()
    load_do.start()

    barrier = pltpu.get_barrier_semaphore()
    pl.semaphore_signal(barrier, inc=1, device_id=(right, enc), device_id_type=MESH)
    pl.semaphore_signal(barrier, inc=1, device_id=(left, enc), device_id_type=MESH)
    pl.semaphore_signal(barrier, inc=1, device_id=(twin, enc), device_id_type=MESH)

    def greet(i, carry):
        peer = lax.rem(enc + i, n_enc)
        pl.semaphore_signal(barrier, inc=1, device_id=(2 * y, peer), device_id_type=MESH)
        pl.semaphore_signal(barrier, inc=1, device_id=(2 * y + 1, peer), device_id_type=MESH)
        return carry

    lax.fori_loop(1, n_enc, greet, 0)
    pl.semaphore_wait(barrier, 2 * n_enc + 1)

    here = core * n_enc + enc
    keep_in = pltpu.make_async_copy(own_ref.at[enc, core], slots.at[here], in_recv)
    keep_in.start()
    remote(own_ref.at[enc, other], slots.at[here], in_send, in_recv, twin, enc).start()

    def scatter_in(i, carry):
        peer = lax.rem(enc + i, n_enc)
        remote(own_ref.at[peer, 0], slots.at[here], in_send, in_recv, 2 * y, peer).start()
        remote(own_ref.at[peer, 1], slots.at[here], in_send, in_recv, 2 * y + 1, peer).start()
        return carry

    lax.fori_loop(1, n_enc, scatter_in, 0)

    swaps = [
        remote(text_ref, text_buf.at[core], swap_send.at[0], swap_recv.at[0], twin, enc),
        remote(q_ref.at[:, theirs], q_buf.at[core], swap_send.at[1], swap_recv.at[1], twin, enc),
        remote(do_ref.at[:, theirs], do_buf.at[core], swap_send.at[2], swap_recv.at[2], twin, enc),
    ]
    for swap in swaps:
        swap.start()

    pltpu.make_async_copy(slots, slots, in_recv).wait()
    rows[...] = slots[...].astype(F32).reshape(rows.shape)
    for kind in range(2):
        for a in range(HALF_KV):
            lines = rows[pl.ds(kind * HALF_KV + a, tile, stride=2 * HALF_KV), :]
            kv[y, a, kind] = lines.astype(BF16)

    def ag_copy(way, hop, a, block):
        target = right if way == 0 else left
        return remote(
            kv.at[block, a],
            kv.at[block, a],
            ag_send.at[way, hop - 1, a],
            ag_recv.at[way, hop - 1, a],
            target,
            enc,
        )

    def ag_first(a, carry):
        ag_copy(0, 1, a, y).start()
        ag_copy(1, 1, a, y).start()
        return carry

    lax.fori_loop(0, HALF_KV, ag_first, 0)

    text_buf[core] = text_ref[...]
    swaps[0].wait_recv()
    text_row = jnp.concatenate([text_buf[0], text_buf[1]], axis=1)
    for half in range(2):
        spread = jnp.broadcast_to(text_buf[half].astype(F32), (HD, tokens))
        late_mask[half * tokens:(half + 1) * tokens, :] = spread.T.astype(BF16)
    limit = jnp.where(text_row == 0, tiles_ref[0, 0], tiles_ref[0, 1])
    biases = [jnp.where(limit > t, 0.0, big_negative).astype(F32) for t in range(MAX_TILES)]
    early = text_row == 0

    for hop in range(1, 4):
        behind = lax.rem(y + RING - hop, RING)
        ahead = lax.rem(y + hop, RING)

        def ag_step(a, carry, hop=hop, behind=behind, ahead=ahead):
            ag_copy(0, hop, a, behind).wait_recv()
            ag_copy(1, hop, a, ahead).wait_recv()
            if hop < 3:
                ag_copy(0, hop + 1, a, behind).start()
                ag_copy(1, hop + 1, a, ahead).start()
            return carry

        lax.fori_loop(0, HALF_KV, ag_step, 0)
        if hop == 3:
            for a in range(2):
                ag_copy(0, 4, a, behind).start()
                ag_copy(1, 4, a + 2, ahead).start()

    load_q.wait()
    load_do.wait()
    swaps[1].wait_recv()
    swaps[2].wait_recv()

    far = lax.rem(y + 4, RING)

    def rs_copy(way, hop, a):
        target = right if way == 0 else left
        return remote(
            rs_send.at[way, hop - 1, a],
            rs_recv.at[way, hop - 1, a],
            red_send.at[way, hop - 1, a],
            red_recv.at[way, hop - 1, a],
            target,
            enc,
        )

    def head(a, carry):
        remote(
            kv.at[far, a], kv.at[far, a], ag_send.at[a // 2, 3, a], ag_recv.at[a // 2, 3, a], right, enc
        ).wait_recv()
        keys = jnp.concatenate(
            [kv[0:MAX_TILES, a, 0].reshape(span, HD), kv[MAX_TILES:RING, a, 0].reshape(span, HD)], axis=1
        )
        values = jnp.concatenate(
            [kv[0:MAX_TILES, a, 1].reshape(span, HD), kv[MAX_TILES:RING, a, 1].reshape(span, HD)], axis=1
        )
        keys_t = keys.T
        late = late_mask[...]
        for r in range(RATIO):
            cols = pl.ds(pl.multiple_of((a * RATIO + r) * HD, HD), HD)
            block = slice(r * 2 * tokens, (r + 1) * 2 * tokens)
            q = q_buf[:, :, cols].reshape(2 * tokens, HD)
            q_late = q * late
            qc = jnp.concatenate([q - q_late, q_late], axis=1)
            d = do_buf[:, :, cols].reshape(2 * tokens, HD)
            d_late = d * late
            dc = jnp.concatenate([d - d_late, d_late], axis=1)
            qc_all[block, :] = qc
            dc_all[block, :] = dc
            s = nt_dot(keys, qc)
            g = nt_dot(values, dc)
            s = jnp.concatenate(
                [s[t * tile:(t + 1) * tile] + biases[t] for t in range(MAX_TILES)], axis=0
            )
            top = jnp.max(s, axis=0, keepdims=True)
            e = jnp.exp2((s - top) * EXP2_SCALE)
            inv = 1.0 / jnp.sum(e, axis=0, keepdims=True)
            row_dot = jnp.sum(e * g, axis=0, keepdims=True) * inv
            p_all[:, block] = (e * inv).astype(BF16)
            ds = (e * ((g - row_dot) * (inv * SCALE))).astype(BF16)
            ds_all[:, block] = ds
            both = jnp.dot(keys_t, ds, preferred_element_type=F32)
            dq = jnp.where(early, both[:HD], both[HD:]).T.astype(BF16)
            dq_buf[:, :, cols] = dq.reshape(2, tokens, HD)
        dk = jnp.dot(ds_all[...], qc_all[...], preferred_element_type=F32)
        dv = jnp.dot(p_all[...], dc_all[...], preferred_element_type=F32)
        for sample in range(SAMP):
            for t in range(MAX_TILES):
                window = (slice(t * tile, (t + 1) * tile), slice(sample * HD, (sample + 1) * HD))
                part[a, sample * MAX_TILES + t, 0] = dk[window]
                part[a, sample * MAX_TILES + t, 1] = dv[window]
        hop_r = 4 - a // 2
        hop_l = 3 + a // 2
        rs_send[0, hop_r - 1, a] = part[a, lax.rem(y + hop_r, RING)].astype(BF16)
        rs_copy(0, hop_r, a).start()
        rs_send[1, hop_l - 1, a] = part[a, lax.rem(y + RING - hop_l, RING)].astype(BF16)
        rs_copy(1, hop_l, a).start()
        return carry

    lax.fori_loop(0, HALF_KV, head, 0)

    dq_keep = pltpu.make_async_copy(dq_buf.at[core], dq_ref.at[:, mine], dq_sem)
    dq_keep.start()
    dq_swap = remote(dq_buf.at[other], dq_ref.at[:, mine], dq_send, dq_recv, twin, enc)
    dq_swap.start()

    def rs_add(way, hop, a):
        rs_copy(way, hop + 1, a).wait_recv()
        dest = lax.rem(y + hop, RING) if way == 0 else lax.rem(y + RING - hop, RING)
        total = part[a, dest] + rs_recv[way, hop, a].astype(F32)
        rs_send[way, hop - 1, a] = total.astype(BF16)
        rs_copy(way, hop, a).start()

    for a in range(2):
        rs_add(0, 3, a)
        rs_add(1, 3, a + 2)
    for hop in (2, 1):

        def rs_step(a, carry, hop=hop):
            rs_add(0, hop, a)
            rs_add(1, hop, a)
            return carry

        lax.fori_loop(0, HALF_KV, rs_step, 0)

    for a in range(HALF_KV):
        rs_copy(0, 1, a).wait_recv()
        rs_copy(1, 1, a).wait_recv()
        total = part[a, y] + rs_recv[0, 0, a].astype(F32) + rs_recv[1, 0, a].astype(F32)
        for kind in range(2):
            rows[pl.ds(kind * HALF_KV + a, tile, stride=2 * HALF_KV), :] = total[kind]

    pltpu.make_async_copy(slots.at[pl.ds(0, tile - 1)], slots.at[pl.ds(0, tile - 1)], in_send).wait()
    slots[...] = rows[...].reshape(slots.shape).astype(BF16)
    keep_out = pltpu.make_async_copy(slots.at[here], dkv_ref.at[enc, core], out_recv)
    keep_out.start()
    remote(
        slots.at[other * n_enc + enc], dkv_ref.at[enc, core], out_send, out_recv, twin, enc
    ).start()

    def scatter_out(i, carry):
        peer = lax.rem(enc + i, n_enc)
        remote(slots.at[peer], dkv_ref.at[enc, core], out_send, out_recv, 2 * y, peer).start()
        remote(slots.at[n_enc + peer], dkv_ref.at[enc, core], out_send, out_recv, 2 * y + 1, peer).start()
        return carry

    lax.fori_loop(1, n_enc, scatter_out, 0)

    for swap in swaps:
        swap.wait_send()

    def drain(a, carry):
        for way in range(2):
            for hop in range(1, 4):
                ag_copy(way, hop, a, y).wait_send()
                rs_copy(way, hop, a).wait_send()
        remote(
            kv.at[far, a], kv.at[far, a], ag_send.at[a // 2, 3, a], ag_recv.at[a // 2, 3, a], right, enc
        ).wait_send()
        remote(
            rs_send.at[a // 2, 3, a],
            rs_recv.at[a // 2, 3, a],
            red_send.at[a // 2, 3, a],
            red_recv.at[a // 2, 3, a],
            right,
            enc,
        ).wait_send()
        return carry

    lax.fori_loop(0, HALF_KV, drain, 0)
    dq_keep.wait()
    dq_swap.wait()
    pltpu.make_async_copy(slots.at[pl.ds(0, tile - 1)], slots.at[pl.ds(0, tile - 1)], out_send).wait()
    pltpu.make_async_copy(dkv_ref, dkv_ref, out_recv).wait()


def shards(n_enc, queries, d_out, text_sample, tiles, img_k, img_v):
    tokens, width = queries.shape[1:]
    tile = 2 * n_enc
    span = MAX_TILES * tile
    rows = HALF_KV * 2
    own = jnp.concatenate(
        [img_k.reshape(n_enc, 2, HALF_KV, HD), img_v.reshape(n_enc, 2, HALF_KV, HD)], axis=2
    )
    vmem = pl.BlockSpec(memory_space=pltpu.VMEM)
    anywhere = pl.BlockSpec(memory_space=pl.ANY)
    dma = pltpu.SemaphoreType.DMA
    d_queries, d_own = pl.pallas_call(
        functools.partial(kernel, n_enc),
        out_shape=(
            jax.ShapeDtypeStruct((tokens, width), BF16),
            jax.ShapeDtypeStruct((n_enc, 2, rows, HD), BF16),
        ),
        in_specs=[pl.BlockSpec(memory_space=pltpu.SMEM), vmem, anywhere, anywhere, anywhere],
        out_specs=(anywhere, anywhere),
        scratch_shapes=[
            pltpu.VMEM((2, 1, tokens), jnp.int32),
            pltpu.VMEM((2 * tokens, HD), BF16),
            pltpu.VMEM((2, tokens, width // 2), BF16),
            pltpu.VMEM((2, tokens, width // 2), BF16),
            pltpu.VMEM((2, tokens, width // 2), BF16),
            pltpu.VMEM((tile, rows, HD), BF16),
            pltpu.VMEM((tile * rows, HD), F32),
            pltpu.VMEM((RING, HALF_KV, 2, tile, HD), BF16),
            pltpu.VMEM((span, RATIO * 2 * tokens), BF16),
            pltpu.VMEM((span, RATIO * 2 * tokens), BF16),
            pltpu.VMEM((RATIO * 2 * tokens, 2 * HD), BF16),
            pltpu.VMEM((RATIO * 2 * tokens, 2 * HD), BF16),
            pltpu.VMEM((HALF_KV, RING, 2, tile, HD), F32),
            pltpu.VMEM((2, 4, HALF_KV, 2, tile, HD), BF16),
            pltpu.VMEM((2, 4, HALF_KV, 2, tile, HD), BF16),
            dma((2,)),
            dma((3,)),
            dma((3,)),
            dma,
            dma,
            dma((2, 4, HALF_KV)),
            dma((2, 4, HALF_KV)),
            dma((2, 4, HALF_KV)),
            dma((2, 4, HALF_KV)),
            dma,
            dma,
            dma,
            dma,
            dma,
        ],
        compiler_params=pltpu.CompilerParams(
            collective_id=0, has_side_effects=True, vmem_limit_bytes=40 * 1024 * 1024
        ),
    )(tiles, text_sample, own, queries[0], d_out[0])
    back_keys = d_own[:, :, :HALF_KV].reshape(n_enc, 1, KVH * HD)
    back_values = d_own[:, :, HALF_KV:].reshape(n_enc, 1, KVH * HD)
    return (d_queries[None], back_keys, back_values)


def solution(mesh):
    in_specs = (
        P("enc", "ctx", None),
        P("enc", "ctx", None),
        P("enc", "ctx"),
        P("enc", None),
        P(None, ("ctx", "enc"), None),
        P(None, ("ctx", "enc"), None),
    )
    out_specs = (
        P("enc", "ctx", None),
        P(None, ("ctx", "enc"), None),
        P(None, ("ctx", "enc"), None),
    )
    return jax.shard_map(
        functools.partial(shards, mesh.shape["enc"]),
        mesh=mesh,
        in_specs=in_specs,
        out_specs=out_specs,
        check_vma=False,
    )
```

```python
import functools
import math

import jax
import jax.numpy as jnp
from jax import lax
from jax.experimental import pallas as pl
from jax.experimental.pallas import tpu as pltpu
from jax.sharding import PartitionSpec as P

H = 32
KVH = 8
HD = 128
SAMP = 2
MAX_TILES = 4
RING = SAMP * MAX_TILES
HALF_KV = KVH // 2
RATIO = H // KVH
SCALE = HD ** -0.5
EXP2_SCALE = SCALE * math.log2(math.e)

big_negative = -1e30
VMEM_LIMIT = 58 * 1024 * 1024

MESH = pl.DeviceIdType.MESH
F32 = jnp.float32
BF16 = jnp.bfloat16


def remote(src, dst, send_sem, recv_sem, ctx, enc):
    return pltpu.make_async_remote_copy(
        src_ref=src,
        dst_ref=dst,
        send_sem=send_sem,
        recv_sem=recv_sem,
        device_id=(ctx, enc),
        device_id_type=MESH,
    )


def peer_of(n_enc, enc, i):
    if n_enc != 32:
        return lax.rem(enc + i + 1, n_enc)
    far_z = i // 4
    near = (far_z + 1) // 2
    z = lax.rem(enc // 4 + 12 + near - 2 * near * lax.rem(far_z + 1, 2), 8)
    far_x = lax.rem(i, 4)
    x = lax.rem(enc + 2 + far_x + far_x // 2 * (1 - 2 * lax.rem(far_x, 2)), 4)
    return 4 * z + x


def nt_dot(a, b):
    return lax.dot_general(a, b, (((1,), (1,)), ((), ())), preferred_element_type=F32)


def kernel(
    n_enc,
    tiles_hbm,
    text_hbm,
    k_ref,
    v_ref,
    q_ref,
    do_ref,
    dq_ref,
    dkv_ref,
    tiles_ref,
    text_buf,
    kv_in,
    own_ref,
    late_mask,
    q_buf,
    do_buf,
    dq_buf,
    slots,
    rows,
    kv,
    ds_all,
    p_all,
    qc_all,
    dc_all,
    part,
    rs_send,
    rs_recv,
    load_sem,
    swap_send,
    swap_recv,
    in_send,
    in_recv,
    ag_send,
    ag_recv,
    red_send,
    red_recv,
    out_send,
    out_recv,
    dq_sem,
    dq_send,
    dq_recv,
    small_sem,
):
    ctx = lax.axis_index("ctx")
    enc = lax.axis_index("enc")
    y = ctx // 2
    core = lax.rem(ctx, 2)
    other = 1 - core
    twin = 2 * y + other
    ahead = [2 * lax.rem(y + step, RING) + core for step in (1, 2)]
    behind = [2 * lax.rem(y + RING - step, RING) + core for step in (1, 2)]
    along = [ahead, behind]
    tokens = q_ref.shape[0]
    width = q_ref.shape[1] // 2
    tile = 2 * n_enc
    span = MAX_TILES * tile

    mine = pl.ds(pl.multiple_of(core * width, width), width)
    theirs = pl.ds(pl.multiple_of(other * width, width), width)

    barrier = pltpu.get_barrier_semaphore()
    pl.semaphore_signal(barrier, inc=1, device_id=(twin, enc), device_id_type=MESH)
    for step in range(2):
        pl.semaphore_signal(barrier, inc=1, device_id=(ahead[step], enc), device_id_type=MESH)
        pl.semaphore_signal(barrier, inc=1, device_id=(behind[step], enc), device_id_type=MESH)

    def greet(i, carry):
        peer = peer_of(n_enc, enc, i)
        pl.semaphore_signal(barrier, inc=1, device_id=(2 * y, peer), device_id_type=MESH)
        pl.semaphore_signal(barrier, inc=1, device_id=(2 * y + 1, peer), device_id_type=MESH)
        return carry

    lax.fori_loop(0, n_enc - 1, greet, 0)
    load_k = pltpu.make_async_copy(k_ref, kv_in.at[0], small_sem.at[0])
    load_v = pltpu.make_async_copy(v_ref, kv_in.at[1], small_sem.at[1])
    load_tiles = pltpu.make_async_copy(tiles_hbm, tiles_ref, small_sem.at[2])
    load_text = pltpu.make_async_copy(text_hbm, text_buf.at[core], small_sem.at[3])
    load_q = pltpu.make_async_copy(q_ref.at[:, mine], q_buf.at[core], load_sem.at[0])
    load_do = pltpu.make_async_copy(do_ref.at[:, mine], do_buf.at[core], load_sem.at[1])
    loads = [load_k, load_v, load_tiles, load_text, load_q, load_do]
    for load in loads:
        load.start()

    load_k.wait()
    load_v.wait()
    for kind in range(2):
        for h in range(KVH):
            first = h // HALF_KV * 2 * HALF_KV + kind * HALF_KV + h % HALF_KV
            piece = kv_in[kind, :, h * HD:(h + 1) * HD]
            rows[pl.ds(first, n_enc, stride=4 * HALF_KV), :] = piece.astype(F32)
    own_ref[...] = rows[...].reshape(own_ref.shape).astype(BF16)

    pl.semaphore_wait(barrier, 2 * n_enc + 3)

    here = core * n_enc + enc
    def scatter_in(i, carry):
        peer = peer_of(n_enc, enc, i)
        remote(own_ref.at[peer, 0], slots.at[here], in_send, in_recv, 2 * y, peer).start()
        remote(own_ref.at[peer, 1], slots.at[here], in_send, in_recv, 2 * y + 1, peer).start()
        return carry

    lax.fori_loop(0, n_enc - 1, scatter_in, 0)

    keep_in = pltpu.make_async_copy(own_ref.at[enc, core], slots.at[here], in_recv)
    keep_in.start()
    remote(own_ref.at[enc, other], slots.at[here], in_send, in_recv, twin, enc).start()

    swaps = [
        remote(text_hbm, text_buf.at[core], swap_send.at[0], swap_recv.at[0], twin, enc),
        remote(q_ref.at[:, theirs], q_buf.at[core], swap_send.at[1], swap_recv.at[1], twin, enc),
        remote(do_ref.at[:, theirs], do_buf.at[core], swap_send.at[2], swap_recv.at[2], twin, enc),
    ]
    for swap in swaps:
        swap.start()

    pltpu.make_async_copy(slots, slots, in_recv).wait()
    rows[...] = slots[...].astype(F32).reshape(rows.shape)
    for kind in range(2):
        for a in range(HALF_KV):
            lines = rows[pl.ds(kind * HALF_KV + a, tile, stride=2 * HALF_KV), :]
            kv[y, a, kind] = lines.astype(BF16)

    def ag_copy(way, a, offset, step):
        block = lax.rem(y + RING - offset, RING) if way == 0 else lax.rem(y + offset, RING)
        sem = offset + step - 1
        return remote(
            kv.at[block, a], kv.at[block, a], ag_send.at[way, sem, a], ag_recv.at[way, sem, a], along[way][step - 1], enc
        )

    def ag_wait(way, a, offset):
        block = lax.rem(y + RING - offset, RING) if way == 0 else lax.rem(y + offset, RING)
        sem = offset - 1
        remote(
            kv.at[block, a], kv.at[block, a], ag_send.at[way, sem, a], ag_recv.at[way, sem, a], along[way][0], enc
        ).wait_recv()

    for step in (2, 1):

        def ag_first(a, carry, step=step):
            ag_copy(0, a, 0, step).start()
            ag_copy(1, a, 0, step).start()
            return carry

        lax.fori_loop(0, HALF_KV, ag_first, 0)

    load_tiles.wait()
    load_text.wait()
    swaps[0].wait_recv()
    text_row = jnp.concatenate([text_buf[0], text_buf[1]], axis=1)
    for half in range(2):
        spread = jnp.broadcast_to(text_buf[half].astype(F32), (HD, tokens))
        late_mask[half * tokens:(half + 1) * tokens, :] = spread.T.astype(BF16)
    limit = jnp.where(text_row == 0, tiles_ref[0, 0], tiles_ref[0, 1])
    biases = [jnp.where(limit > t, 0.0, big_negative).astype(F32) for t in range(MAX_TILES)]
    early = text_row == 0

    for a in range(HALF_KV):
        for way in range(2):
            ag_wait(way, a, 2)
            if way == a // 2:
                ag_copy(way, a, 2, 2).start()
            ag_copy(way, a, 2, 1).start()

    load_q.wait()
    load_do.wait()
    swaps[1].wait_recv()
    swaps[2].wait_recv()

    far = lax.rem(y + 4, RING)

    def far_copy(a):
        side = a // 2
        return remote(
            kv.at[far, a], kv.at[far, a], ag_send.at[side, 3, a], ag_recv.at[side, 3, a], along[0][0], enc
        )

    def rs_copy(way, kind, a, target):
        return remote(
            rs_send.at[way, kind, a],
            rs_recv.at[way, kind, a],
            red_send.at[way, kind, a],
            red_recv.at[way, kind, a],
            target,
            enc,
        )

    def due(way, steps):
        return lax.rem(y + steps, RING) if way == 0 else lax.rem(y + RING - steps, RING)

    def rs_first(a):
        side = a // 2
        rs_send[side, 1, a] = part[a, far].astype(BF16)
        rs_copy(side, 1, a, ahead[1] + side * (behind[1] - ahead[1])).start()
        for way in range(2):
            rs_send[way, 0, a] = part[a, due(way, 3)].astype(BF16)
            rs_copy(way, 0, a, along[way][0]).start()
        for way in range(2):
            rs_send[way, 2, a] = part[a, due(way, 1)].astype(BF16)
            rs_copy(way, 2, a, along[way][0]).start()

    def rs_second(a, side):
        for way in range(2):
            total = part[a, due(way, 2)]
            rs_copy(way, 0, a, along[way][0]).wait_recv()
            total = total + rs_recv[way, 0, a].astype(F32)
            if way == side:
                rs_copy(way, 1, a, along[way][0]).wait_recv()
                total = total + rs_recv[way, 1, a].astype(F32)
            rs_send[way, 3, a] = total.astype(BF16)
            rs_copy(way, 3, a, along[way][1]).start()

    def head(a, carry):
        for way in range(2):
            ag_wait(way, a, 1)
            ag_wait(way, a, 3)
        far_copy(a).wait_recv()
        keys = jnp.concatenate(
            [kv[0:MAX_TILES, a, 0].reshape(span, HD), kv[MAX_TILES:RING, a, 0].reshape(span, HD)], axis=1
        )
        values = jnp.concatenate(
            [kv[0:MAX_TILES, a, 1].reshape(span, HD), kv[MAX_TILES:RING, a, 1].reshape(span, HD)], axis=1
        )
        keys_t = keys.T
        late = late_mask[...]
        for r in range(RATIO):
            cols = pl.ds(pl.multiple_of((a * RATIO + r) * HD, HD), HD)
            block = slice(r * 2 * tokens, (r + 1) * 2 * tokens)
            q = q_buf[:, :, cols].reshape(2 * tokens, HD)
            q_late = q * late
            qc = jnp.concatenate([q - q_late, q_late], axis=1)
            d = do_buf[:, :, cols].reshape(2 * tokens, HD)
            d_late = d * late
            dc = jnp.concatenate([d - d_late, d_late], axis=1)
            qc_all[block, :] = qc
            dc_all[block, :] = dc
            s = nt_dot(keys, qc)
            g = nt_dot(values, dc)
            s = jnp.concatenate(
                [s[t * tile:(t + 1) * tile] + biases[t] for t in range(MAX_TILES)], axis=0
            )
            top = jnp.max(s, axis=0, keepdims=True)
            e = jnp.exp2((s - top) * EXP2_SCALE)
            inv = 1.0 / jnp.sum(e, axis=0, keepdims=True)
            row_dot = jnp.sum(e * g, axis=0, keepdims=True) * inv
            p_all[:, block] = (e * inv).astype(BF16)
            ds = (e * ((g - row_dot) * (inv * SCALE))).astype(BF16)
            ds_all[:, block] = ds
            both = jnp.dot(keys_t, ds, preferred_element_type=F32)
            dq = jnp.where(early, both[:HD], both[HD:]).T.astype(BF16)
            dq_buf[:, :, cols] = dq.reshape(2, tokens, HD)
        dk = jnp.dot(ds_all[...], qc_all[...], preferred_element_type=F32)
        dv = jnp.dot(p_all[...], dc_all[...], preferred_element_type=F32)
        for sample in range(SAMP):
            for t in range(MAX_TILES):
                window = (slice(t * tile, (t + 1) * tile), slice(sample * HD, (sample + 1) * HD))
                part[a, sample * MAX_TILES + t, 0] = dk[window]
                part[a, sample * MAX_TILES + t, 1] = dv[window]
        rs_first(a)

        @pl.when(a >= 2)
        def _():
            rs_second(a - 2, 0)

        return carry

    lax.fori_loop(0, HALF_KV, head, 0)

    dq_keep = pltpu.make_async_copy(dq_buf.at[core], dq_ref.at[:, mine], dq_sem)
    dq_keep.start()
    dq_swap = remote(dq_buf.at[other], dq_ref.at[:, mine], dq_send, dq_recv, twin, enc)
    dq_swap.start()

    rs_second(2, 1)
    rs_second(3, 1)

    for a in range(HALF_KV):
        total = part[a, y]
        for way in range(2):
            for kind in (2, 3):
                rs_copy(way, kind, a, along[way][0]).wait_recv()
                total = total + rs_recv[way, kind, a].astype(F32)
        for kind in range(2):
            rows[pl.ds(kind * HALF_KV + a, tile, stride=2 * HALF_KV), :] = total[kind]

    pltpu.make_async_copy(slots.at[pl.ds(0, tile - 1)], slots.at[pl.ds(0, tile - 1)], in_send).wait()
    slots[...] = rows[...].reshape(slots.shape).astype(BF16)
    def scatter_out(i, carry):
        peer = peer_of(n_enc, enc, i)
        remote(slots.at[peer], dkv_ref.at[enc, core], out_send, out_recv, 2 * y, peer).start()
        remote(slots.at[n_enc + peer], dkv_ref.at[enc, core], out_send, out_recv, 2 * y + 1, peer).start()
        return carry

    lax.fori_loop(0, n_enc - 1, scatter_out, 0)

    keep_out = pltpu.make_async_copy(slots.at[here], dkv_ref.at[enc, core], out_recv)
    keep_out.start()
    remote(
        slots.at[other * n_enc + enc], dkv_ref.at[enc, core], out_send, out_recv, twin, enc
    ).start()

    for swap in swaps:
        swap.wait_send()

    def drain(a, carry):
        for way in range(2):
            ag_copy(way, a, 0, 1).wait_send()
            ag_copy(way, a, 0, 2).wait_send()
            ag_copy(way, a, 2, 1).wait_send()
            for kind in (0, 2, 3):
                rs_copy(way, kind, a, along[way][0]).wait_send()
        far_copy(a).wait_send()
        rs_copy(a // 2, 1, a, along[0][0]).wait_send()
        return carry

    lax.fori_loop(0, HALF_KV, drain, 0)
    dq_keep.wait()
    dq_swap.wait()
    pltpu.make_async_copy(slots.at[pl.ds(0, tile - 1)], slots.at[pl.ds(0, tile - 1)], out_send).wait()
    pltpu.make_async_copy(dkv_ref, dkv_ref, out_recv).wait()


def finish(n_enc, dq_ref, dkv_ref, dq_out, k_out, v_out, rows, sem):
    keep = pltpu.make_async_copy(dq_ref, dq_out, sem)
    keep.start()
    rows[...] = dkv_ref[...].astype(F32).reshape(rows.shape)
    for kind, out in enumerate((k_out, v_out)):
        for h in range(KVH):
            first = h // HALF_KV * 2 * HALF_KV + kind * HALF_KV + h % HALF_KV
            out[:, h * HD:(h + 1) * HD] = rows[pl.ds(first, n_enc, stride=4 * HALF_KV), :].astype(BF16)
    keep.wait()


def shards(n_enc, queries, d_out, text_sample, tiles, img_k, img_v):
    tokens, width = queries.shape[1:]
    tile = 2 * n_enc
    span = MAX_TILES * tile
    rows = HALF_KV * 2
    vmem = pl.BlockSpec(memory_space=pltpu.VMEM)
    anywhere = pl.BlockSpec(memory_space=pl.ANY)
    dma = pltpu.SemaphoreType.DMA
    d_queries, d_own = pl.pallas_call(
        functools.partial(kernel, n_enc),
        out_shape=(
            pltpu.VMEM((tokens, width), BF16),
            pltpu.VMEM((n_enc, 2, rows, HD), BF16),
        ),
        in_specs=[anywhere] * 6,
        out_specs=(anywhere, anywhere),
        scratch_shapes=[
            pltpu.SMEM((1, SAMP), jnp.int32),
            pltpu.VMEM((2, 1, tokens), jnp.int32),
            pltpu.VMEM((2, n_enc, KVH * HD), BF16),
            pltpu.VMEM((n_enc, 2, rows, HD), BF16),
            pltpu.VMEM((2 * tokens, HD), BF16),
            pltpu.VMEM((2, tokens, width // 2), BF16),
            pltpu.VMEM((2, tokens, width // 2), BF16),
            pltpu.VMEM((2, tokens, width // 2), BF16),
            pltpu.VMEM((tile, rows, HD), BF16),
            pltpu.VMEM((tile * rows, HD), F32),
            pltpu.VMEM((RING, HALF_KV, 2, tile, HD), BF16),
            pltpu.VMEM((span, RATIO * 2 * tokens), BF16),
            pltpu.VMEM((span, RATIO * 2 * tokens), BF16),
            pltpu.VMEM((RATIO * 2 * tokens, 2 * HD), BF16),
            pltpu.VMEM((RATIO * 2 * tokens, 2 * HD), BF16),
            pltpu.VMEM((HALF_KV, RING, 2, tile, HD), F32),
            pltpu.VMEM((2, 4, HALF_KV, 2, tile, HD), BF16),
            pltpu.VMEM((2, 4, HALF_KV, 2, tile, HD), BF16),
            dma((2,)),
            dma((3,)),
            dma((3,)),
            dma,
            dma,
            dma((2, 4, HALF_KV)),
            dma((2, 4, HALF_KV)),
            dma((2, 4, HALF_KV)),
            dma((2, 4, HALF_KV)),
            dma,
            dma,
            dma,
            dma,
            dma,
            dma((4,)),
        ],
        compiler_params=pltpu.CompilerParams(
            collective_id=0, has_side_effects=True, vmem_limit_bytes=VMEM_LIMIT
        ),
    )(
        tiles,
        text_sample,
        img_k.reshape(n_enc, KVH * HD),
        img_v.reshape(n_enc, KVH * HD),
        queries[0],
        d_out[0],
    )
    d_queries, back_keys, back_values = pl.pallas_call(
        functools.partial(finish, n_enc),
        out_shape=(
            jax.ShapeDtypeStruct((tokens, width), BF16),
            jax.ShapeDtypeStruct((n_enc, KVH * HD), BF16),
            jax.ShapeDtypeStruct((n_enc, KVH * HD), BF16),
        ),
        in_specs=[vmem, vmem],
        out_specs=(anywhere, vmem, vmem),
        scratch_shapes=[
            pltpu.VMEM((n_enc * 2 * rows, HD), F32),
            dma,
        ],
        compiler_params=pltpu.CompilerParams(vmem_limit_bytes=VMEM_LIMIT // 4),
    )(d_queries, d_own)
    return (
        d_queries[None],
        back_keys.reshape(n_enc, 1, KVH * HD),
        back_values.reshape(n_enc, 1, KVH * HD),
    )


def solution(mesh):
    in_specs = (
        P("enc", "ctx", None),
        P("enc", "ctx", None),
        P("enc", "ctx"),
        P("enc", None),
        P(None, ("ctx", "enc"), None),
        P(None, ("ctx", "enc"), None),
    )
    out_specs = (
        P("enc", "ctx", None),
        P(None, ("ctx", "enc"), None),
        P(None, ("ctx", "enc"), None),
    )
    return jax.shard_map(
        functools.partial(shards, mesh.shape["enc"]),
        mesh=mesh,
        in_specs=in_specs,
        out_specs=out_specs,
        check_vma=False,
    )
```

```python
import functools
import math

import jax
import jax.numpy as jnp
from jax import lax
from jax.experimental import pallas as pl
from jax.experimental.pallas import tpu as pltpu
from jax.sharding import PartitionSpec as P

H = 32
KVH = 8
HD = 128
SAMP = 2
MAX_TILES = 4
RING = SAMP * MAX_TILES
HALF_KV = KVH // 2
RATIO = H // KVH
SCALE = HD ** -0.5
EXP2_SCALE = SCALE * math.log2(math.e)

big_negative = -1e30
VMEM_LIMIT = 58 * 1024 * 1024
LONG_FROM = 2

MESH = pl.DeviceIdType.MESH
F32 = jnp.float32
BF16 = jnp.bfloat16


def remote(src, dst, send_sem, recv_sem, ctx, enc):
    return pltpu.make_async_remote_copy(
        src_ref=src,
        dst_ref=dst,
        send_sem=send_sem,
        recv_sem=recv_sem,
        device_id=(ctx, enc),
        device_id_type=MESH,
    )


def each_peer(n_enc, enc, visit):
    n_x = min(4, n_enc)
    n_z = n_enc // n_x
    z, x = enc // n_x, lax.rem(enc, n_x)
    columns = [lax.rem(x + step, n_x) for step in sorted(range(1, n_x), key=lambda step: -min(step, n_x - step))]

    def plane(i, carry):
        near = (i + 1) // 2
        row = lax.rem(z + n_z + n_z // 2 + near - 2 * near * lax.rem(i + 1, 2), n_z) * n_x
        for column in columns + [x]:
            visit(row + column)
        return carry

    if n_z > 1:
        lax.fori_loop(0, n_z - 1, plane, 0)
    for column in columns:
        visit(z * n_x + column)


def nt_dot(a, b):
    return lax.dot_general(a, b, (((1,), (1,)), ((), ())), preferred_element_type=F32)


def kernel(
    n_enc,
    tiles_hbm,
    text_hbm,
    k_ref,
    v_ref,
    q_ref,
    do_ref,
    dq_ref,
    dkv_ref,
    tiles_ref,
    text_buf,
    kv_in,
    own_ref,
    late_mask,
    q_buf,
    do_buf,
    dq_buf,
    slots,
    rows,
    kv,
    scores,
    grads,
    ds_all,
    qc_all,
    dc_all,
    part,
    rs_send,
    rs_recv,
    load_sem,
    swap_send,
    swap_recv,
    in_send,
    in_recv,
    ag_send,
    ag_recv,
    red_send,
    red_recv,
    out_send,
    out_recv,
    dq_sem,
    dq_send,
    dq_recv,
    small_sem,
):
    ctx = lax.axis_index("ctx")
    enc = lax.axis_index("enc")
    y = ctx // 2
    core = lax.rem(ctx, 2)
    other = 1 - core
    twin = 2 * y + other
    ahead = [2 * lax.rem(y + step, RING) + core for step in (1, 2)]
    behind = [2 * lax.rem(y + RING - step, RING) + core for step in (1, 2)]
    along = [ahead, behind]
    tokens = q_ref.shape[0]
    width = q_ref.shape[1] // 2
    tile = 2 * n_enc
    span = MAX_TILES * tile

    mine = pl.ds(pl.multiple_of(core * width, width), width)
    theirs = pl.ds(pl.multiple_of(other * width, width), width)

    load_k = pltpu.make_async_copy(k_ref, kv_in.at[0], small_sem.at[0])
    load_v = pltpu.make_async_copy(v_ref, kv_in.at[1], small_sem.at[1])
    load_tiles = pltpu.make_async_copy(tiles_hbm, tiles_ref, small_sem.at[2])
    load_text = pltpu.make_async_copy(text_hbm, text_buf.at[core], small_sem.at[3])
    load_q = pltpu.make_async_copy(q_ref.at[:, mine], q_buf.at[core], load_sem.at[0])
    load_do = pltpu.make_async_copy(do_ref.at[:, mine], do_buf.at[core], load_sem.at[1])
    loads = [load_k, load_v, load_tiles, load_text, load_q, load_do]
    for load in loads:
        load.start()

    barrier = pltpu.get_barrier_semaphore()
    pl.semaphore_signal(barrier, inc=1, device_id=(twin, enc), device_id_type=MESH)
    for step in range(2):
        pl.semaphore_signal(barrier, inc=1, device_id=(ahead[step], enc), device_id_type=MESH)
        pl.semaphore_signal(barrier, inc=1, device_id=(behind[step], enc), device_id_type=MESH)

    def greet(peer):
        pl.semaphore_signal(barrier, inc=1, device_id=(2 * y, peer), device_id_type=MESH)
        pl.semaphore_signal(barrier, inc=1, device_id=(2 * y + 1, peer), device_id_type=MESH)

    each_peer(n_enc, enc, greet)

    load_k.wait()
    load_v.wait()
    for kind in range(2):
        for h in range(KVH):
            first = h // HALF_KV * 2 * HALF_KV + kind * HALF_KV + h % HALF_KV
            piece = kv_in[kind, :, h * HD:(h + 1) * HD]
            rows[pl.ds(first, n_enc, stride=4 * HALF_KV), :] = piece.astype(F32)
    own_ref[...] = rows[...].reshape(own_ref.shape).astype(BF16)

    pl.semaphore_wait(barrier, 2 * n_enc + 3)

    here = core * n_enc + enc
    def scatter_in(peer):
        remote(own_ref.at[peer, 0], slots.at[here], in_send, in_recv, 2 * y, peer).start()
        remote(own_ref.at[peer, 1], slots.at[here], in_send, in_recv, 2 * y + 1, peer).start()

    each_peer(n_enc, enc, scatter_in)
    keep_in = pltpu.make_async_copy(own_ref.at[enc, core], slots.at[here], in_recv)
    keep_in.start()
    remote(own_ref.at[enc, other], slots.at[here], in_send, in_recv, twin, enc).start()

    swaps = [
        remote(text_hbm, text_buf.at[core], swap_send.at[0], swap_recv.at[0], twin, enc),
        remote(q_ref.at[:, theirs], q_buf.at[core], swap_send.at[1], swap_recv.at[1], twin, enc),
        remote(do_ref.at[:, theirs], do_buf.at[core], swap_send.at[2], swap_recv.at[2], twin, enc),
    ]
    for swap in swaps:
        swap.start()

    pltpu.make_async_copy(slots, slots, in_recv).wait()
    rows[...] = slots[...].astype(F32).reshape(rows.shape)
    for kind in range(2):
        for a in range(HALF_KV):
            lines = rows[pl.ds(kind * HALF_KV + a, tile, stride=2 * HALF_KV), :]
            kv[y, a, kind] = lines.astype(BF16)

    def ag_copy(way, a, offset, step):
        block = lax.rem(y + RING - offset, RING) if way == 0 else lax.rem(y + offset, RING)
        sem = offset + step - 1
        return remote(
            kv.at[block, a], kv.at[block, a], ag_send.at[way, sem, a], ag_recv.at[way, sem, a], along[way][step - 1], enc
        )

    def ag_wait(way, a, offset):
        block = lax.rem(y + RING - offset, RING) if way == 0 else lax.rem(y + offset, RING)
        sem = offset - 1
        remote(
            kv.at[block, a], kv.at[block, a], ag_send.at[way, sem, a], ag_recv.at[way, sem, a], along[way][0], enc
        ).wait_recv()

    def ag_first(a, carry):
        ag_copy(0, a, 0, 1).start()
        ag_copy(1, a, 0, 1).start()
        return carry

    lax.fori_loop(0, HALF_KV, ag_first, 0)

    load_tiles.wait()
    load_text.wait()
    swaps[0].wait_recv()
    text_row = jnp.concatenate([text_buf[0], text_buf[1]], axis=1)
    for half in range(2):
        spread = jnp.broadcast_to(text_buf[half].astype(F32), (HD, tokens))
        late_mask[half * tokens:(half + 1) * tokens, :] = spread.T.astype(BF16)
    limit = jnp.where(text_row == 0, tiles_ref[0, 0], tiles_ref[0, 1])
    biases = [jnp.where(limit > t, 0.0, big_negative).astype(F32) for t in range(MAX_TILES)]
    early = text_row == 0

    for a in range(HALF_KV):
        for way in range(2):
            ag_wait(way, a, 1)
            ag_copy(way, a, 1, 1).start()
    for a in range(HALF_KV):
        for way in range(2):
            ag_wait(way, a, 2)
            if way == a // 2:
                ag_copy(way, a, 2, 2).start()
            ag_copy(way, a, 2, 1).start()

    load_q.wait()
    load_do.wait()
    swaps[1].wait_recv()
    swaps[2].wait_recv()

    def spread_heads(h, carry):
        cols = pl.ds(pl.multiple_of(h * HD, HD), HD)
        late = late_mask[...]
        for source, target in ((q_buf, qc_all), (do_buf, dc_all)):
            every = source[:, :, cols].reshape(2 * tokens, HD)
            second = every * late
            target[h, :, :HD] = every - second
            target[h, :, HD:] = second
        return carry

    lax.fori_loop(0, HALF_KV * RATIO, spread_heads, 0)

    far = lax.rem(y + 4, RING)

    def far_copy(a):
        side = a // 2
        return remote(
            kv.at[far, a], kv.at[far, a], ag_send.at[side, 3, a], ag_recv.at[side, 3, a], along[0][0], enc
        )

    def rs_copy(way, kind, a, target):
        return remote(
            rs_send.at[way, kind, a],
            rs_recv.at[way, kind, a],
            red_send.at[way, kind, a],
            red_recv.at[way, kind, a],
            target,
            enc,
        )

    def due(way, steps):
        return lax.rem(y + steps, RING) if way == 0 else lax.rem(y + RING - steps, RING)

    def rs_first(a):
        side = a // 2
        rs_send[side, 1, a] = part[a, far].astype(BF16)
        rs_copy(side, 1, a, ahead[1] + side * (behind[1] - ahead[1])).start()
        for way in range(2):
            rs_send[way, 0, a] = part[a, due(way, 3)].astype(BF16)
            rs_copy(way, 0, a, along[way][0]).start()

        @pl.when(a >= LONG_FROM)
        def _():
            for way in range(2):
                rs_send[way, 2, a] = part[a, due(way, 1)].astype(BF16)
                rs_copy(way, 2, a, along[way][0]).start()

    def rs_second(a, side, steps):
        for way in range(2):
            total = part[a, due(way, 2)]
            rs_copy(way, 0, a, along[way][0]).wait_recv()
            total = total + rs_recv[way, 0, a].astype(F32)
            if way == side:
                rs_copy(way, 1, a, along[way][0]).wait_recv()
                total = total + rs_recv[way, 1, a].astype(F32)
            rs_send[way, 3, a] = total.astype(BF16)
            rs_copy(way, 3, a, along[way][steps - 1]).start()

    def rs_third(a):
        for way in range(2):
            rs_copy(way, 3, a, along[way][0]).wait_recv()
            total = part[a, due(way, 1)] + rs_recv[way, 3, a].astype(F32)
            rs_send[way, 2, a] = total.astype(BF16)
            rs_copy(way, 2, a, along[way][0]).start()

    def head(a, carry):
        for way in range(2):
            ag_wait(way, a, 3)
        far_copy(a).wait_recv()
        keys = jnp.concatenate(
            [kv[0:MAX_TILES, a, 0].reshape(span, HD), kv[MAX_TILES:RING, a, 0].reshape(span, HD)], axis=1
        )
        values = jnp.concatenate(
            [kv[0:MAX_TILES, a, 1].reshape(span, HD), kv[MAX_TILES:RING, a, 1].reshape(span, HD)], axis=1
        )
        for r in range(RATIO):
            scores[r] = nt_dot(keys, qc_all[a * RATIO + r])
            grads[r] = nt_dot(values, dc_all[a * RATIO + r])
        dk = jnp.zeros((span, 2 * HD), F32)
        dv = jnp.zeros((span, 2 * HD), F32)
        for r in range(RATIO):
            s = scores[r]
            g = grads[r]
            s = jnp.concatenate(
                [s[t * tile:(t + 1) * tile] + biases[t] for t in range(MAX_TILES)], axis=0
            )
            top = jnp.max(s, axis=0, keepdims=True)
            e = jnp.exp2((s - top) * EXP2_SCALE)
            inv = 1.0 / jnp.sum(e, axis=0, keepdims=True)
            row_dot = jnp.sum(e * g, axis=0, keepdims=True) * inv
            p = (e * inv).astype(BF16)
            ds = (e * ((g - row_dot) * (inv * SCALE))).astype(BF16)
            ds_all[a * RATIO + r] = ds
            dk = dk + jnp.dot(ds, qc_all[a * RATIO + r], preferred_element_type=F32)
            dv = dv + jnp.dot(p, dc_all[a * RATIO + r], preferred_element_type=F32)
        for sample in range(SAMP):
            for t in range(MAX_TILES):
                window = (slice(t * tile, (t + 1) * tile), slice(sample * HD, (sample + 1) * HD))
                part[a, sample * MAX_TILES + t, 0] = dk[window]
                part[a, sample * MAX_TILES + t, 1] = dv[window]
        rs_first(a)

        @pl.when(a >= 2)
        def _():
            rs_second(a - 2, 0, 1)

        return carry

    lax.fori_loop(0, HALF_KV, head, 0)

    def query_grads(a, carry):
        keys_t = jnp.concatenate(
            [kv[0:MAX_TILES, a, 0].reshape(span, HD), kv[MAX_TILES:RING, a, 0].reshape(span, HD)], axis=1
        ).T
        for r in range(RATIO):
            cols = pl.ds(pl.multiple_of((a * RATIO + r) * HD, HD), HD)
            both = jnp.dot(keys_t, ds_all[a * RATIO + r], preferred_element_type=F32)
            dq = jnp.where(early, both[:HD], both[HD:]).T.astype(BF16)
            dq_buf[:, :, cols] = dq.reshape(2, tokens, HD)
        return carry

    lax.fori_loop(0, HALF_KV // 2, query_grads, 0)
    rs_second(2, 1, 1 if LONG_FROM > 2 else 2)
    rs_third(0)
    lax.fori_loop(HALF_KV // 2, HALF_KV, query_grads, 0)
    rs_second(3, 1, 1 if LONG_FROM > 3 else 2)
    rs_third(1)
    for a in range(2, LONG_FROM):
        rs_third(a)
    dq_keep = pltpu.make_async_copy(dq_buf.at[core], dq_ref.at[:, mine], dq_sem)
    dq_keep.start()
    dq_swap = remote(dq_buf.at[other], dq_ref.at[:, mine], dq_send, dq_recv, twin, enc)
    dq_swap.start()

    for a in range(HALF_KV):
        total = part[a, y]
        for way in range(2):
            for kind in (2, 3) if a >= LONG_FROM else (2,):
                rs_copy(way, kind, a, along[way][0]).wait_recv()
                total = total + rs_recv[way, kind, a].astype(F32)
        for kind in range(2):
            rows[pl.ds(kind * HALF_KV + a, tile, stride=2 * HALF_KV), :] = total[kind]

    pltpu.make_async_copy(slots.at[pl.ds(0, tile - 1)], slots.at[pl.ds(0, tile - 1)], in_send).wait()
    slots[...] = rows[...].reshape(slots.shape).astype(BF16)
    def scatter_out(peer):
        remote(slots.at[peer], dkv_ref.at[enc, core], out_send, out_recv, 2 * y, peer).start()
        remote(slots.at[n_enc + peer], dkv_ref.at[enc, core], out_send, out_recv, 2 * y + 1, peer).start()

    each_peer(n_enc, enc, scatter_out)
    keep_out = pltpu.make_async_copy(slots.at[here], dkv_ref.at[enc, core], out_recv)
    keep_out.start()
    remote(
        slots.at[other * n_enc + enc], dkv_ref.at[enc, core], out_send, out_recv, twin, enc
    ).start()

    for swap in swaps:
        swap.wait_send()

    def drain(a, carry):
        for way in range(2):
            ag_copy(way, a, 0, 1).wait_send()
            ag_copy(way, a, 0, 2).wait_send()
            ag_copy(way, a, 2, 1).wait_send()
            for kind in (0, 2, 3):
                rs_copy(way, kind, a, along[way][0]).wait_send()
        far_copy(a).wait_send()
        rs_copy(a // 2, 1, a, along[0][0]).wait_send()
        return carry

    lax.fori_loop(0, HALF_KV, drain, 0)
    dq_keep.wait()
    dq_swap.wait()
    pltpu.make_async_copy(slots.at[pl.ds(0, tile - 1)], slots.at[pl.ds(0, tile - 1)], out_send).wait()
    pltpu.make_async_copy(dkv_ref, dkv_ref, out_recv).wait()


def finish(n_enc, dq_ref, dkv_ref, dq_out, k_out, v_out, rows, k_rows, v_rows, sem):
    half = dq_ref.shape[0] // 2
    copies = [
        pltpu.make_async_copy(dq_ref.at[pl.ds(i * half, half)], dq_out.at[pl.ds(i * half, half)], sem.at[i])
        for i in range(2)
    ]
    for copy in copies:
        copy.start()
    rows[...] = dkv_ref[...].astype(F32).reshape(rows.shape)
    for kind, (lines, out) in enumerate(((k_rows, k_out), (v_rows, v_out))):
        for h in range(KVH):
            first = h // HALF_KV * 2 * HALF_KV + kind * HALF_KV + h % HALF_KV
            lines[:, h * HD:(h + 1) * HD] = rows[pl.ds(first, n_enc, stride=4 * HALF_KV), :].astype(BF16)
        copies.append(pltpu.make_async_copy(lines, out, sem.at[2 + kind]))
        copies[-1].start()
    for copy in copies:
        copy.wait()


def shards(n_enc, queries, d_out, text_sample, tiles, img_k, img_v):
    tokens, width = queries.shape[1:]
    tile = 2 * n_enc
    span = MAX_TILES * tile
    rows = HALF_KV * 2
    vmem = pl.BlockSpec(memory_space=pltpu.VMEM)
    anywhere = pl.BlockSpec(memory_space=pl.ANY)
    dma = pltpu.SemaphoreType.DMA
    d_queries, d_own = pl.pallas_call(
        functools.partial(kernel, n_enc),
        out_shape=(
            pltpu.VMEM((tokens, width), BF16),
            pltpu.VMEM((n_enc, 2, rows, HD), BF16),
        ),
        in_specs=[anywhere] * 6,
        out_specs=(anywhere, anywhere),
        scratch_shapes=[
            pltpu.SMEM((1, SAMP), jnp.int32),
            pltpu.VMEM((2, 1, tokens), jnp.int32),
            pltpu.VMEM((2, n_enc, KVH * HD), BF16),
            pltpu.VMEM((n_enc, 2, rows, HD), BF16),
            pltpu.VMEM((2 * tokens, HD), BF16),
            pltpu.VMEM((2, tokens, width // 2), BF16),
            pltpu.VMEM((2, tokens, width // 2), BF16),
            pltpu.VMEM((2, tokens, width // 2), BF16),
            pltpu.VMEM((tile, rows, HD), BF16),
            pltpu.VMEM((tile * rows, HD), F32),
            pltpu.VMEM((RING, HALF_KV, 2, tile, HD), BF16),
            pltpu.VMEM((RATIO, span, 2 * tokens), F32),
            pltpu.VMEM((RATIO, span, 2 * tokens), F32),
            pltpu.VMEM((HALF_KV * RATIO, span, 2 * tokens), BF16),
            pltpu.VMEM((HALF_KV * RATIO, 2 * tokens, 2 * HD), BF16),
            pltpu.VMEM((HALF_KV * RATIO, 2 * tokens, 2 * HD), BF16),
            pltpu.VMEM((HALF_KV, RING, 2, tile, HD), F32),
            pltpu.VMEM((2, 4, HALF_KV, 2, tile, HD), BF16),
            pltpu.VMEM((2, 4, HALF_KV, 2, tile, HD), BF16),
            dma((2,)),
            dma((3,)),
            dma((3,)),
            dma,
            dma,
            dma((2, 4, HALF_KV)),
            dma((2, 4, HALF_KV)),
            dma((2, 4, HALF_KV)),
            dma((2, 4, HALF_KV)),
            dma,
            dma,
            dma,
            dma,
            dma,
            dma((4,)),
        ],
        compiler_params=pltpu.CompilerParams(
            collective_id=0, has_side_effects=True, vmem_limit_bytes=VMEM_LIMIT
        ),
    )(
        tiles,
        text_sample,
        img_k.reshape(n_enc, KVH * HD),
        img_v.reshape(n_enc, KVH * HD),
        queries[0],
        d_out[0],
    )
    d_queries, back_keys, back_values = pl.pallas_call(
        functools.partial(finish, n_enc),
        out_shape=(
            jax.ShapeDtypeStruct((tokens, width), BF16),
            jax.ShapeDtypeStruct((n_enc, KVH * HD), BF16),
            jax.ShapeDtypeStruct((n_enc, KVH * HD), BF16),
        ),
        in_specs=[vmem, vmem],
        out_specs=(anywhere, anywhere, anywhere),
        scratch_shapes=[
            pltpu.VMEM((n_enc * 2 * rows, HD), F32),
            pltpu.VMEM((n_enc, KVH * HD), BF16),
            pltpu.VMEM((n_enc, KVH * HD), BF16),
            dma((4,)),
        ],
        compiler_params=pltpu.CompilerParams(vmem_limit_bytes=VMEM_LIMIT // 4),
    )(d_queries, d_own)
    return (
        d_queries[None],
        back_keys.reshape(n_enc, 1, KVH * HD),
        back_values.reshape(n_enc, 1, KVH * HD),
    )


def solution(mesh):
    in_specs = (
        P("enc", "ctx", None),
        P("enc", "ctx", None),
        P("enc", "ctx"),
        P("enc", None),
        P(None, ("ctx", "enc"), None),
        P(None, ("ctx", "enc"), None),
    )
    out_specs = (
        P("enc", "ctx", None),
        P(None, ("ctx", "enc"), None),
        P(None, ("ctx", "enc"), None),
    )
    return jax.shard_map(
        functools.partial(shards, mesh.shape["enc"]),
        mesh=mesh,
        in_specs=in_specs,
        out_specs=out_specs,
        check_vma=False,
    )
```

```python
import functools
import math

import jax
import jax.numpy as jnp
from jax import lax
from jax.experimental import pallas as pl
from jax.experimental.pallas import tpu as pltpu
from jax.sharding import PartitionSpec as P

H = 32
KVH = 8
HD = 128
SAMP = 2
MAX_TILES = 4
RING = SAMP * MAX_TILES
HALF_KV = KVH // 2
RATIO = H // KVH
SCALE = HD ** -0.5
EXP2_SCALE = SCALE * math.log2(math.e)

big_negative = -1e30
VMEM_LIMIT = 58 * 1024 * 1024
LONG_FROM = 3

MESH = pl.DeviceIdType.MESH
F32 = jnp.float32
BF16 = jnp.bfloat16


def remote(src, dst, send_sem, recv_sem, ctx, enc):
    return pltpu.make_async_remote_copy(
        src_ref=src,
        dst_ref=dst,
        send_sem=send_sem,
        recv_sem=recv_sem,
        device_id=(ctx, enc),
        device_id_type=MESH,
    )


def each_peer(n_enc, enc, visit):
    n_x = min(4, n_enc)
    n_z = n_enc // n_x
    z, x = enc // n_x, lax.rem(enc, n_x)
    columns = [lax.rem(x + step, n_x) for step in sorted(range(1, n_x), key=lambda step: -min(step, n_x - step))]

    def plane(i, carry):
        near = (i + 1) // 2
        row = lax.rem(z + n_z + n_z // 2 + near - 2 * near * lax.rem(i + 1, 2), n_z) * n_x
        for column in columns + [x]:
            visit(row + column)
        return carry

    if n_z > 1:
        lax.fori_loop(0, n_z - 1, plane, 0)
    for column in columns:
        visit(z * n_x + column)


def side_of(a):
    return a % 2 if isinstance(a, int) else lax.rem(a, 2)


def nt_dot(a, b):
    return lax.dot_general(a, b, (((1,), (1,)), ((), ())), preferred_element_type=F32)


def kernel(
    n_enc,
    tiles_hbm,
    text_hbm,
    k_ref,
    v_ref,
    q_ref,
    do_ref,
    dq_ref,
    dkv_ref,
    tiles_ref,
    text_buf,
    kv_in,
    own_ref,
    late_mask,
    q_buf,
    do_buf,
    dq_buf,
    slots,
    rows,
    kv,
    scores,
    grads,
    ds_all,
    qc_all,
    dc_all,
    part,
    rs_send,
    rs_recv,
    load_sem,
    swap_send,
    swap_recv,
    in_send,
    in_recv,
    ag_send,
    ag_recv,
    red_send,
    red_recv,
    out_send,
    out_recv,
    dq_sem,
    dq_send,
    dq_recv,
    small_sem,
):
    ctx = lax.axis_index("ctx")
    enc = lax.axis_index("enc")
    y = ctx // 2
    core = lax.rem(ctx, 2)
    other = 1 - core
    twin = 2 * y + other
    ahead = [2 * lax.rem(y + step, RING) + core for step in (1, 2)]
    behind = [2 * lax.rem(y + RING - step, RING) + core for step in (1, 2)]
    along = [ahead, behind]
    tokens = q_ref.shape[0]
    width = q_ref.shape[1] // 2
    tile = 2 * n_enc
    span = MAX_TILES * tile

    mine = pl.ds(pl.multiple_of(core * width, width), width)
    theirs = pl.ds(pl.multiple_of(other * width, width), width)

    load_k = pltpu.make_async_copy(k_ref, kv_in.at[0], small_sem.at[0])
    load_v = pltpu.make_async_copy(v_ref, kv_in.at[1], small_sem.at[1])
    load_tiles = pltpu.make_async_copy(tiles_hbm, tiles_ref, small_sem.at[2])
    load_text = pltpu.make_async_copy(text_hbm, text_buf.at[core], small_sem.at[3])
    load_q = pltpu.make_async_copy(q_ref.at[:, mine], q_buf.at[core], load_sem.at[0])
    load_do = pltpu.make_async_copy(do_ref.at[:, mine], do_buf.at[core], load_sem.at[1])
    loads = [load_k, load_v, load_tiles, load_text, load_q, load_do]
    for load in loads:
        load.start()

    barrier = pltpu.get_barrier_semaphore()
    pl.semaphore_signal(barrier, inc=1, device_id=(twin, enc), device_id_type=MESH)
    for step in range(2):
        pl.semaphore_signal(barrier, inc=1, device_id=(ahead[step], enc), device_id_type=MESH)
        pl.semaphore_signal(barrier, inc=1, device_id=(behind[step], enc), device_id_type=MESH)

    def greet(peer):
        pl.semaphore_signal(barrier, inc=1, device_id=(2 * y, peer), device_id_type=MESH)
        pl.semaphore_signal(barrier, inc=1, device_id=(2 * y + 1, peer), device_id_type=MESH)

    each_peer(n_enc, enc, greet)

    load_k.wait()
    load_v.wait()
    for kind in range(2):
        for h in range(KVH):
            first = h // HALF_KV * 2 * HALF_KV + kind * HALF_KV + h % HALF_KV
            piece = kv_in[kind, :, h * HD:(h + 1) * HD]
            rows[pl.ds(first, n_enc, stride=4 * HALF_KV), :] = piece.astype(F32)
    own_ref[...] = rows[...].reshape(own_ref.shape).astype(BF16)

    pl.semaphore_wait(barrier, 2 * n_enc + 3)

    here = core * n_enc + enc
    def scatter_in(peer):
        remote(own_ref.at[peer, 0], slots.at[here], in_send, in_recv, 2 * y, peer).start()
        remote(own_ref.at[peer, 1], slots.at[here], in_send, in_recv, 2 * y + 1, peer).start()

    each_peer(n_enc, enc, scatter_in)
    keep_in = pltpu.make_async_copy(own_ref.at[enc, core], slots.at[here], in_recv)
    keep_in.start()
    remote(own_ref.at[enc, other], slots.at[here], in_send, in_recv, twin, enc).start()

    swaps = [
        remote(text_hbm, text_buf.at[core], swap_send.at[0], swap_recv.at[0], twin, enc),
        remote(q_ref.at[:, theirs], q_buf.at[core], swap_send.at[1], swap_recv.at[1], twin, enc),
        remote(do_ref.at[:, theirs], do_buf.at[core], swap_send.at[2], swap_recv.at[2], twin, enc),
    ]
    for swap in swaps:
        swap.start()

    pltpu.make_async_copy(slots, slots, in_recv).wait()
    rows[...] = slots[...].astype(F32).reshape(rows.shape)
    for kind in range(2):
        for a in range(HALF_KV):
            lines = rows[pl.ds(kind * HALF_KV + a, tile, stride=2 * HALF_KV), :]
            kv[y, a, kind] = lines.astype(BF16)

    def ag_copy(way, a, offset, step):
        block = lax.rem(y + RING - offset, RING) if way == 0 else lax.rem(y + offset, RING)
        sem = offset + step - 1
        return remote(
            kv.at[block, a], kv.at[block, a], ag_send.at[way, sem, a], ag_recv.at[way, sem, a], along[way][step - 1], enc
        )

    def ag_wait(way, a, offset):
        block = lax.rem(y + RING - offset, RING) if way == 0 else lax.rem(y + offset, RING)
        sem = offset - 1
        remote(
            kv.at[block, a], kv.at[block, a], ag_send.at[way, sem, a], ag_recv.at[way, sem, a], along[way][0], enc
        ).wait_recv()

    def ag_first(a, carry):
        ag_copy(0, a, 0, 1).start()
        ag_copy(1, a, 0, 1).start()
        return carry

    lax.fori_loop(0, HALF_KV, ag_first, 0)

    load_tiles.wait()
    load_text.wait()
    swaps[0].wait_recv()
    text_row = jnp.concatenate([text_buf[0], text_buf[1]], axis=1)
    for half in range(2):
        spread = jnp.broadcast_to(text_buf[half].astype(F32), (HD, tokens))
        late_mask[half * tokens:(half + 1) * tokens, :] = spread.T.astype(BF16)
    limit = jnp.where(text_row == 0, tiles_ref[0, 0], tiles_ref[0, 1])
    biases = [jnp.where(limit > t, 0.0, big_negative).astype(F32) for t in range(MAX_TILES)]
    early = text_row == 0

    for a in range(HALF_KV):
        for way in range(2):
            ag_wait(way, a, 1)
            ag_copy(way, a, 1, 1).start()
    for a in range(HALF_KV):
        for way in range(2):
            ag_wait(way, a, 2)
            if way == side_of(a):
                ag_copy(way, a, 2, 2).start()
            ag_copy(way, a, 2, 1).start()

    load_q.wait()
    load_do.wait()
    swaps[1].wait_recv()
    swaps[2].wait_recv()

    def spread_heads(h, carry):
        cols = pl.ds(pl.multiple_of(h * HD, HD), HD)
        late = late_mask[...]
        for source, target in ((q_buf, qc_all), (do_buf, dc_all)):
            every = source[:, :, cols].reshape(2 * tokens, HD)
            second = every * late
            target[h, :, :HD] = every - second
            target[h, :, HD:] = second
        return carry

    lax.fori_loop(0, HALF_KV * RATIO, spread_heads, 0)

    far = lax.rem(y + 4, RING)

    def far_copy(a):
        side = side_of(a)
        return remote(
            kv.at[far, a], kv.at[far, a], ag_send.at[side, 3, a], ag_recv.at[side, 3, a], along[0][0], enc
        )

    def rs_copy(way, kind, a, target):
        return remote(
            rs_send.at[way, kind, a],
            rs_recv.at[way, kind, a],
            red_send.at[way, kind, a],
            red_recv.at[way, kind, a],
            target,
            enc,
        )

    def due(way, steps):
        return lax.rem(y + steps, RING) if way == 0 else lax.rem(y + RING - steps, RING)

    def rs_first(a):
        side = side_of(a)
        rs_send[side, 1, a] = part[a, far].astype(BF16)
        rs_copy(side, 1, a, ahead[1] + side * (behind[1] - ahead[1])).start()
        for way in range(2):
            rs_send[way, 0, a] = part[a, due(way, 3)].astype(BF16)
            rs_copy(way, 0, a, along[way][0]).start()

        @pl.when(a >= LONG_FROM)
        def _():
            for way in range(2):
                rs_send[way, 2, a] = part[a, due(way, 1)].astype(BF16)
                rs_copy(way, 2, a, along[way][0]).start()

    def rs_second(a):
        side = side_of(a)
        steps = 1 if a < LONG_FROM else 2
        for way in range(2):
            total = part[a, due(way, 2)]
            rs_copy(way, 0, a, along[way][0]).wait_recv()
            total = total + rs_recv[way, 0, a].astype(F32)
            if way == side:
                rs_copy(way, 1, a, along[way][0]).wait_recv()
                total = total + rs_recv[way, 1, a].astype(F32)
            rs_send[way, 3, a] = total.astype(BF16)
            rs_copy(way, 3, a, along[way][steps - 1]).start()

    def rs_third(a):
        for way in range(2):
            rs_copy(way, 3, a, along[way][0]).wait_recv()
            total = part[a, due(way, 1)] + rs_recv[way, 3, a].astype(F32)
            rs_send[way, 2, a] = total.astype(BF16)
            rs_copy(way, 2, a, along[way][0]).start()

    def head(a, carry):
        for way in range(2):
            ag_wait(way, a, 3)
        far_copy(a).wait_recv()
        keys = jnp.concatenate(
            [kv[0:MAX_TILES, a, 0].reshape(span, HD), kv[MAX_TILES:RING, a, 0].reshape(span, HD)], axis=1
        )
        values = jnp.concatenate(
            [kv[0:MAX_TILES, a, 1].reshape(span, HD), kv[MAX_TILES:RING, a, 1].reshape(span, HD)], axis=1
        )
        for r in range(RATIO):
            scores[r] = nt_dot(keys, qc_all[a * RATIO + r])
            grads[r] = nt_dot(values, dc_all[a * RATIO + r])
        dk = jnp.zeros((span, 2 * HD), F32)
        dv = jnp.zeros((span, 2 * HD), F32)
        for r in range(RATIO):
            s = scores[r]
            g = grads[r]
            s = jnp.concatenate(
                [s[t * tile:(t + 1) * tile] + biases[t] for t in range(MAX_TILES)], axis=0
            )
            top = jnp.max(s, axis=0, keepdims=True)
            e = jnp.exp2((s - top) * EXP2_SCALE)
            inv = 1.0 / jnp.sum(e, axis=0, keepdims=True)
            row_dot = jnp.sum(e * g, axis=0, keepdims=True) * inv
            p = (e * inv).astype(BF16)
            ds = (e * ((g - row_dot) * (inv * SCALE))).astype(BF16)
            ds_all[a * RATIO + r] = ds
            dk = dk + jnp.dot(ds, qc_all[a * RATIO + r], preferred_element_type=F32)
            dv = dv + jnp.dot(p, dc_all[a * RATIO + r], preferred_element_type=F32)
        for sample in range(SAMP):
            for t in range(MAX_TILES):
                window = (slice(t * tile, (t + 1) * tile), slice(sample * HD, (sample + 1) * HD))
                part[a, sample * MAX_TILES + t, 0] = dk[window]
                part[a, sample * MAX_TILES + t, 1] = dv[window]
        rs_first(a)

        return carry

    lax.fori_loop(0, HALF_KV, head, 0)

    def query_grads(a, carry):
        keys_t = jnp.concatenate(
            [kv[0:MAX_TILES, a, 0].reshape(span, HD), kv[MAX_TILES:RING, a, 0].reshape(span, HD)], axis=1
        ).T
        for r in range(RATIO):
            cols = pl.ds(pl.multiple_of((a * RATIO + r) * HD, HD), HD)
            both = jnp.dot(keys_t, ds_all[a * RATIO + r], preferred_element_type=F32)
            dq = jnp.where(early, both[:HD], both[HD:]).T.astype(BF16)
            dq_buf[:, :, cols] = dq.reshape(2, tokens, HD)
        return carry

    lax.fori_loop(0, HALF_KV // 2, query_grads, 0)
    rs_second(0)
    rs_second(1)
    lax.fori_loop(HALF_KV // 2, HALF_KV, query_grads, 0)
    rs_second(2)
    rs_third(0)
    rs_second(3)
    rs_third(1)
    rs_third(2)

    dq_keep = pltpu.make_async_copy(dq_buf.at[core], dq_ref.at[:, mine], dq_sem)
    dq_keep.start()
    dq_swap = remote(dq_buf.at[other], dq_ref.at[:, mine], dq_send, dq_recv, twin, enc)
    dq_swap.start()

    for a in range(HALF_KV):
        total = part[a, y]
        for way in range(2):
            for kind in (2, 3) if a >= LONG_FROM else (2,):
                rs_copy(way, kind, a, along[way][0]).wait_recv()
                total = total + rs_recv[way, kind, a].astype(F32)
        for kind in range(2):
            rows[pl.ds(kind * HALF_KV + a, tile, stride=2 * HALF_KV), :] = total[kind]

    pltpu.make_async_copy(slots.at[pl.ds(0, tile - 1)], slots.at[pl.ds(0, tile - 1)], in_send).wait()
    slots[...] = rows[...].reshape(slots.shape).astype(BF16)
    def scatter_out(peer):
        remote(slots.at[peer], dkv_ref.at[enc, core], out_send, out_recv, 2 * y, peer).start()
        remote(slots.at[n_enc + peer], dkv_ref.at[enc, core], out_send, out_recv, 2 * y + 1, peer).start()

    each_peer(n_enc, enc, scatter_out)
    keep_out = pltpu.make_async_copy(slots.at[here], dkv_ref.at[enc, core], out_recv)
    keep_out.start()
    remote(
        slots.at[other * n_enc + enc], dkv_ref.at[enc, core], out_send, out_recv, twin, enc
    ).start()

    for swap in swaps:
        swap.wait_send()

    def drain(a, carry):
        for way in range(2):
            ag_copy(way, a, 0, 1).wait_send()
            ag_copy(way, a, 0, 2).wait_send()
            ag_copy(way, a, 2, 1).wait_send()
            for kind in (0, 2, 3):
                rs_copy(way, kind, a, along[way][0]).wait_send()
        far_copy(a).wait_send()
        rs_copy(side_of(a), 1, a, along[0][0]).wait_send()
        return carry

    lax.fori_loop(0, HALF_KV, drain, 0)
    dq_keep.wait()
    dq_swap.wait()
    pltpu.make_async_copy(slots.at[pl.ds(0, tile - 1)], slots.at[pl.ds(0, tile - 1)], out_send).wait()
    pltpu.make_async_copy(dkv_ref, dkv_ref, out_recv).wait()


def finish(n_enc, dq_ref, dkv_ref, dq_out, k_out, v_out, rows, k_rows, v_rows, sem):
    half = dq_ref.shape[0] // 2
    copies = [
        pltpu.make_async_copy(dq_ref.at[pl.ds(i * half, half)], dq_out.at[pl.ds(i * half, half)], sem.at[i])
        for i in range(2)
    ]
    for copy in copies:
        copy.start()
    rows[...] = dkv_ref[...].astype(F32).reshape(rows.shape)
    for kind, (lines, out) in enumerate(((k_rows, k_out), (v_rows, v_out))):
        for h in range(KVH):
            first = h // HALF_KV * 2 * HALF_KV + kind * HALF_KV + h % HALF_KV
            lines[:, h * HD:(h + 1) * HD] = rows[pl.ds(first, n_enc, stride=4 * HALF_KV), :].astype(BF16)
        copies.append(pltpu.make_async_copy(lines, out, sem.at[2 + kind]))
        copies[-1].start()
    for copy in copies:
        copy.wait()


def shards(n_enc, queries, d_out, text_sample, tiles, img_k, img_v):
    tokens, width = queries.shape[1:]
    tile = 2 * n_enc
    span = MAX_TILES * tile
    rows = HALF_KV * 2
    vmem = pl.BlockSpec(memory_space=pltpu.VMEM)
    anywhere = pl.BlockSpec(memory_space=pl.ANY)
    dma = pltpu.SemaphoreType.DMA
    d_queries, d_own = pl.pallas_call(
        functools.partial(kernel, n_enc),
        out_shape=(
            pltpu.VMEM((tokens, width), BF16),
            pltpu.VMEM((n_enc, 2, rows, HD), BF16),
        ),
        in_specs=[anywhere] * 6,
        out_specs=(anywhere, anywhere),
        scratch_shapes=[
            pltpu.SMEM((1, SAMP), jnp.int32),
            pltpu.VMEM((2, 1, tokens), jnp.int32),
            pltpu.VMEM((2, n_enc, KVH * HD), BF16),
            pltpu.VMEM((n_enc, 2, rows, HD), BF16),
            pltpu.VMEM((2 * tokens, HD), BF16),
            pltpu.VMEM((2, tokens, width // 2), BF16),
            pltpu.VMEM((2, tokens, width // 2), BF16),
            pltpu.VMEM((2, tokens, width // 2), BF16),
            pltpu.VMEM((tile, rows, HD), BF16),
            pltpu.VMEM((tile * rows, HD), F32),
            pltpu.VMEM((RING, HALF_KV, 2, tile, HD), BF16),
            pltpu.VMEM((RATIO, span, 2 * tokens), F32),
            pltpu.VMEM((RATIO, span, 2 * tokens), F32),
            pltpu.VMEM((HALF_KV * RATIO, span, 2 * tokens), BF16),
            pltpu.VMEM((HALF_KV * RATIO, 2 * tokens, 2 * HD), BF16),
            pltpu.VMEM((HALF_KV * RATIO, 2 * tokens, 2 * HD), BF16),
            pltpu.VMEM((HALF_KV, RING, 2, tile, HD), F32),
            pltpu.VMEM((2, 4, HALF_KV, 2, tile, HD), BF16),
            pltpu.VMEM((2, 4, HALF_KV, 2, tile, HD), BF16),
            dma((2,)),
            dma((3,)),
            dma((3,)),
            dma,
            dma,
            dma((2, 4, HALF_KV)),
            dma((2, 4, HALF_KV)),
            dma((2, 4, HALF_KV)),
            dma((2, 4, HALF_KV)),
            dma,
            dma,
            dma,
            dma,
            dma,
            dma((4,)),
        ],
        compiler_params=pltpu.CompilerParams(
            collective_id=0, has_side_effects=True, vmem_limit_bytes=VMEM_LIMIT
        ),
    )(
        tiles,
        text_sample,
        img_k.reshape(n_enc, KVH * HD),
        img_v.reshape(n_enc, KVH * HD),
        queries[0],
        d_out[0],
    )
    d_queries, back_keys, back_values = pl.pallas_call(
        functools.partial(finish, n_enc),
        out_shape=(
            jax.ShapeDtypeStruct((tokens, width), BF16),
            jax.ShapeDtypeStruct((n_enc, KVH * HD), BF16),
            jax.ShapeDtypeStruct((n_enc, KVH * HD), BF16),
        ),
        in_specs=[vmem, vmem],
        out_specs=(anywhere, anywhere, anywhere),
        scratch_shapes=[
            pltpu.VMEM((n_enc * 2 * rows, HD), F32),
            pltpu.VMEM((n_enc, KVH * HD), BF16),
            pltpu.VMEM((n_enc, KVH * HD), BF16),
            dma((4,)),
        ],
        compiler_params=pltpu.CompilerParams(vmem_limit_bytes=VMEM_LIMIT // 4),
    )(d_queries, d_own)
    return (
        d_queries[None],
        back_keys.reshape(n_enc, 1, KVH * HD),
        back_values.reshape(n_enc, 1, KVH * HD),
    )


def solution(mesh):
    in_specs = (
        P("enc", "ctx", None),
        P("enc", "ctx", None),
        P("enc", "ctx"),
        P("enc", None),
        P(None, ("ctx", "enc"), None),
        P(None, ("ctx", "enc"), None),
    )
    out_specs = (
        P("enc", "ctx", None),
        P(None, ("ctx", "enc"), None),
        P(None, ("ctx", "enc"), None),
    )
    return jax.shard_map(
        functools.partial(shards, mesh.shape["enc"]),
        mesh=mesh,
        in_specs=in_specs,
        out_specs=out_specs,
        check_vma=False,
    )
```

```python
import functools
import math

import jax
import jax.numpy as jnp
from jax import lax
from jax.experimental import pallas as pl
from jax.experimental.pallas import tpu as pltpu
from jax.sharding import PartitionSpec as P

H = 32
KVH = 8
HD = 128
SAMP = 2
MAX_TILES = 4
RING = SAMP * MAX_TILES
HALF_KV = KVH // 2
RATIO = H // KVH
SCALE = HD ** -0.5
EXP2_SCALE = SCALE * math.log2(math.e)

big_negative = -1e30
VMEM_LIMIT = 58 * 1024 * 1024
LONG_FROM = 3

MESH = pl.DeviceIdType.MESH
F32 = jnp.float32
BF16 = jnp.bfloat16


def remote(src, dst, send_sem, recv_sem, ctx, enc):
    return pltpu.make_async_remote_copy(
        src_ref=src,
        dst_ref=dst,
        send_sem=send_sem,
        recv_sem=recv_sem,
        device_id=(ctx, enc),
        device_id_type=MESH,
    )


def each_peer(n_enc, enc, visit):
    n_x = min(4, n_enc)
    n_z = n_enc // n_x
    z, x = enc // n_x, lax.rem(enc, n_x)
    columns = [lax.rem(x + step, n_x) for step in sorted(range(1, n_x), key=lambda step: -min(step, n_x - step))]

    def plane(i, carry):
        near = (i + 1) // 2
        row = lax.rem(z + n_z + n_z // 2 + near - 2 * near * lax.rem(i + 1, 2), n_z) * n_x
        for column in columns + [x]:
            visit(row + column)
        return carry

    if n_z > 1:
        lax.fori_loop(0, n_z - 1, plane, 0)
    for column in columns:
        visit(z * n_x + column)


def side_of(a):
    return a % 2 if isinstance(a, int) else lax.rem(a, 2)


def nt_dot(a, b):
    return lax.dot_general(a, b, (((1,), (1,)), ((), ())), preferred_element_type=F32)


def kernel(
    n_enc,
    tiles_hbm,
    text_hbm,
    k_ref,
    v_ref,
    q_ref,
    do_ref,
    dq_ref,
    dkv_ref,
    tiles_ref,
    text_buf,
    kv_in,
    own_ref,
    late_mask,
    q_buf,
    do_buf,
    dq_buf,
    slots,
    rows,
    kv,
    scores,
    grads,
    ds_all,
    qc_all,
    dc_all,
    part,
    rs_send,
    rs_recv,
    load_sem,
    swap_send,
    swap_recv,
    in_send,
    in_recv,
    ag_send,
    ag_recv,
    red_send,
    red_recv,
    out_send,
    out_recv,
    dq_sem,
    dq_send,
    dq_recv,
    small_sem,
):
    ctx = lax.axis_index("ctx")
    enc = lax.axis_index("enc")
    y = ctx // 2
    core = lax.rem(ctx, 2)
    other = 1 - core
    twin = 2 * y + other
    ahead = [2 * lax.rem(y + step, RING) + core for step in (1, 2)]
    behind = [2 * lax.rem(y + RING - step, RING) + core for step in (1, 2)]
    along = [ahead, behind]
    tokens = q_ref.shape[0]
    width = q_ref.shape[1] // 2
    tile = 2 * n_enc
    span = MAX_TILES * tile

    mine = pl.ds(pl.multiple_of(core * width, width), width)
    theirs = pl.ds(pl.multiple_of(other * width, width), width)

    load_k = pltpu.make_async_copy(k_ref, kv_in.at[0], small_sem.at[0])
    load_v = pltpu.make_async_copy(v_ref, kv_in.at[1], small_sem.at[1])
    load_tiles = pltpu.make_async_copy(tiles_hbm, tiles_ref, small_sem.at[2])
    load_text = pltpu.make_async_copy(text_hbm, text_buf.at[core], small_sem.at[3])
    load_q = pltpu.make_async_copy(q_ref.at[:, mine], q_buf.at[core], load_sem.at[0])
    load_do = pltpu.make_async_copy(do_ref.at[:, mine], do_buf.at[core], load_sem.at[1])
    loads = [load_k, load_v, load_tiles, load_text, load_q, load_do]
    for load in loads:
        load.start()

    barrier = pltpu.get_barrier_semaphore()
    pl.semaphore_signal(barrier, inc=1, device_id=(twin, enc), device_id_type=MESH)
    for step in range(2):
        pl.semaphore_signal(barrier, inc=1, device_id=(ahead[step], enc), device_id_type=MESH)
        pl.semaphore_signal(barrier, inc=1, device_id=(behind[step], enc), device_id_type=MESH)

    def greet(peer):
        pl.semaphore_signal(barrier, inc=1, device_id=(2 * y, peer), device_id_type=MESH)
        pl.semaphore_signal(barrier, inc=1, device_id=(2 * y + 1, peer), device_id_type=MESH)

    each_peer(n_enc, enc, greet)

    load_k.wait()
    load_v.wait()
    for kind in range(2):
        for h in range(KVH):
            first = h // HALF_KV * 2 * HALF_KV + kind * HALF_KV + h % HALF_KV
            piece = kv_in[kind, :, h * HD:(h + 1) * HD]
            rows[pl.ds(first, n_enc, stride=4 * HALF_KV), :] = piece.astype(F32)
    own_ref[...] = rows[...].reshape(own_ref.shape).astype(BF16)

    pl.semaphore_wait(barrier, 2 * n_enc + 3)

    here = core * n_enc + enc
    def scatter_in(peer):
        remote(own_ref.at[peer, 0], slots.at[here], in_send, in_recv, 2 * y, peer).start()
        remote(own_ref.at[peer, 1], slots.at[here], in_send, in_recv, 2 * y + 1, peer).start()

    each_peer(n_enc, enc, scatter_in)
    keep_in = pltpu.make_async_copy(own_ref.at[enc, core], slots.at[here], in_recv)
    keep_in.start()
    remote(own_ref.at[enc, other], slots.at[here], in_send, in_recv, twin, enc).start()

    swaps = [
        remote(text_hbm, text_buf.at[core], swap_send.at[0], swap_recv.at[0], twin, enc),
        remote(q_ref.at[:, theirs], q_buf.at[core], swap_send.at[1], swap_recv.at[1], twin, enc),
        remote(do_ref.at[:, theirs], do_buf.at[core], swap_send.at[2], swap_recv.at[2], twin, enc),
    ]
    for swap in swaps:
        swap.start()

    pltpu.make_async_copy(slots, slots, in_recv).wait()
    rows[...] = slots[...].astype(F32).reshape(rows.shape)

    def ag_copy(way, a, offset, step):
        block = lax.rem(y + RING - offset, RING) if way == 0 else lax.rem(y + offset, RING)
        sem = offset + step - 1
        return remote(
            kv.at[block, a], kv.at[block, a], ag_send.at[way, sem, a], ag_recv.at[way, sem, a], along[way][step - 1], enc
        )

    def ag_wait(way, a, offset):
        block = lax.rem(y + RING - offset, RING) if way == 0 else lax.rem(y + offset, RING)
        sem = offset - 1
        remote(
            kv.at[block, a], kv.at[block, a], ag_send.at[way, sem, a], ag_recv.at[way, sem, a], along[way][0], enc
        ).wait_recv()

    for a in range(HALF_KV):
        for kind in range(2):
            lines = rows[pl.ds(kind * HALF_KV + a, tile, stride=2 * HALF_KV), :]
            kv[y, a, kind] = lines.astype(BF16)
        ag_copy(0, a, 0, 1).start()
        ag_copy(1, a, 0, 1).start()

    load_tiles.wait()
    load_text.wait()
    swaps[0].wait_recv()
    text_row = jnp.concatenate([text_buf[0], text_buf[1]], axis=1)
    for half in range(2):
        spread = jnp.broadcast_to(text_buf[half].astype(F32), (HD, tokens))
        late_mask[half * tokens:(half + 1) * tokens, :] = spread.T.astype(BF16)
    limit = jnp.where(text_row == 0, tiles_ref[0, 0], tiles_ref[0, 1])
    biases = [jnp.where(limit > t, 0.0, big_negative).astype(F32) for t in range(MAX_TILES)]
    early = text_row == 0

    for a in range(HALF_KV):
        for way in range(2):
            ag_wait(way, a, 1)
            ag_copy(way, a, 1, 1).start()
    for a in range(HALF_KV):
        for way in range(2):
            ag_wait(way, a, 2)
            if way == side_of(a):
                ag_copy(way, a, 2, 2).start()
            ag_copy(way, a, 2, 1).start()

    load_q.wait()
    load_do.wait()
    swaps[1].wait_recv()
    swaps[2].wait_recv()

    def spread_heads(h, carry):
        cols = pl.ds(pl.multiple_of(h * HD, HD), HD)
        late = late_mask[...]
        for source, target in ((q_buf, qc_all), (do_buf, dc_all)):
            every = source[:, :, cols].reshape(2 * tokens, HD)
            second = every * late
            target[h, :, :HD] = every - second
            target[h, :, HD:] = second
        return carry

    lax.fori_loop(0, HALF_KV * RATIO, spread_heads, 0)

    far = lax.rem(y + 4, RING)

    def far_copy(a):
        side = side_of(a)
        return remote(
            kv.at[far, a], kv.at[far, a], ag_send.at[side, 3, a], ag_recv.at[side, 3, a], along[0][0], enc
        )

    def rs_copy(way, kind, a, target):
        return remote(
            rs_send.at[way, kind, a],
            rs_recv.at[way, kind, a],
            red_send.at[way, kind, a],
            red_recv.at[way, kind, a],
            target,
            enc,
        )

    def due(way, steps):
        return lax.rem(y + steps, RING) if way == 0 else lax.rem(y + RING - steps, RING)

    def rs_first(a):
        side = side_of(a)
        rs_send[side, 1, a] = part[a, far].astype(BF16)
        rs_copy(side, 1, a, ahead[1] + side * (behind[1] - ahead[1])).start()
        for way in range(2):
            rs_send[way, 0, a] = part[a, due(way, 3)].astype(BF16)
            rs_copy(way, 0, a, along[way][0]).start()

        @pl.when(a >= LONG_FROM)
        def _():
            for way in range(2):
                rs_send[way, 2, a] = part[a, due(way, 1)].astype(BF16)
                rs_copy(way, 2, a, along[way][0]).start()

    def rs_second(a):
        side = side_of(a)
        steps = 1 if a < LONG_FROM else 2
        for way in range(2):
            total = part[a, due(way, 2)]
            rs_copy(way, 0, a, along[way][0]).wait_recv()
            total = total + rs_recv[way, 0, a].astype(F32)
            if way == side:
                rs_copy(way, 1, a, along[way][0]).wait_recv()
                total = total + rs_recv[way, 1, a].astype(F32)
            rs_send[way, 3, a] = total.astype(BF16)
            rs_copy(way, 3, a, along[way][steps - 1]).start()

    def rs_third(a):
        for way in range(2):
            rs_copy(way, 3, a, along[way][0]).wait_recv()
            total = part[a, due(way, 1)] + rs_recv[way, 3, a].astype(F32)
            rs_send[way, 2, a] = total.astype(BF16)
            rs_copy(way, 2, a, along[way][0]).start()

    def head(a, carry):
        for way in range(2):
            ag_wait(way, a, 3)
        far_copy(a).wait_recv()
        keys = jnp.concatenate(
            [kv[0:MAX_TILES, a, 0].reshape(span, HD), kv[MAX_TILES:RING, a, 0].reshape(span, HD)], axis=1
        )
        values = jnp.concatenate(
            [kv[0:MAX_TILES, a, 1].reshape(span, HD), kv[MAX_TILES:RING, a, 1].reshape(span, HD)], axis=1
        )
        for r in range(RATIO):
            scores[r] = nt_dot(keys, qc_all[a * RATIO + r])
            grads[r] = nt_dot(values, dc_all[a * RATIO + r])
        dk = jnp.zeros((span, 2 * HD), F32)
        dv = jnp.zeros((span, 2 * HD), F32)
        for r in range(RATIO):
            s = scores[r]
            g = grads[r]
            s = jnp.concatenate(
                [s[t * tile:(t + 1) * tile] + biases[t] for t in range(MAX_TILES)], axis=0
            )
            top = jnp.max(s, axis=0, keepdims=True)
            e = jnp.exp2((s - top) * EXP2_SCALE)
            inv = 1.0 / jnp.sum(e, axis=0, keepdims=True)
            row_dot = jnp.sum(e * g, axis=0, keepdims=True) * inv
            p = (e * inv).astype(BF16)
            ds = (e * ((g - row_dot) * (inv * SCALE))).astype(BF16)
            ds_all[a * RATIO + r] = ds
            dk = dk + jnp.dot(ds, qc_all[a * RATIO + r], preferred_element_type=F32)
            dv = dv + jnp.dot(p, dc_all[a * RATIO + r], preferred_element_type=F32)
        for sample in range(SAMP):
            for t in range(MAX_TILES):
                window = (slice(t * tile, (t + 1) * tile), slice(sample * HD, (sample + 1) * HD))
                part[a, sample * MAX_TILES + t, 0] = dk[window]
                part[a, sample * MAX_TILES + t, 1] = dv[window]
        rs_first(a)

        return carry

    lax.fori_loop(0, HALF_KV, head, 0)

    def query_grads(a, carry):
        keys_t = jnp.concatenate(
            [kv[0:MAX_TILES, a, 0].reshape(span, HD), kv[MAX_TILES:RING, a, 0].reshape(span, HD)], axis=1
        ).T
        for r in range(RATIO):
            cols = pl.ds(pl.multiple_of((a * RATIO + r) * HD, HD), HD)
            both = jnp.dot(keys_t, ds_all[a * RATIO + r], preferred_element_type=F32)
            dq = jnp.where(early, both[:HD], both[HD:]).T.astype(BF16)
            dq_buf[:, :, cols] = dq.reshape(2, tokens, HD)
        return carry

    lax.fori_loop(0, HALF_KV // 2, query_grads, 0)
    rs_second(0)
    rs_second(1)
    lax.fori_loop(HALF_KV // 2, HALF_KV, query_grads, 0)
    rs_second(2)
    rs_third(0)
    rs_second(3)
    rs_third(1)
    rs_third(2)

    dq_keep = pltpu.make_async_copy(dq_buf.at[core], dq_ref.at[:, mine], dq_sem)
    dq_keep.start()
    dq_swap = remote(dq_buf.at[other], dq_ref.at[:, mine], dq_send, dq_recv, twin, enc)
    dq_swap.start()

    for a in range(HALF_KV):
        total = part[a, y]
        for way in range(2):
            for kind in (2, 3) if a >= LONG_FROM else (2,):
                rs_copy(way, kind, a, along[way][0]).wait_recv()
                total = total + rs_recv[way, kind, a].astype(F32)
        for kind in range(2):
            rows[pl.ds(kind * HALF_KV + a, tile, stride=2 * HALF_KV), :] = total[kind]

    pltpu.make_async_copy(slots.at[pl.ds(0, tile - 1)], slots.at[pl.ds(0, tile - 1)], in_send).wait()
    slots[...] = rows[...].reshape(slots.shape).astype(BF16)
    def scatter_out(peer):
        remote(slots.at[peer], dkv_ref.at[enc, core], out_send, out_recv, 2 * y, peer).start()
        remote(slots.at[n_enc + peer], dkv_ref.at[enc, core], out_send, out_recv, 2 * y + 1, peer).start()

    each_peer(n_enc, enc, scatter_out)
    keep_out = pltpu.make_async_copy(slots.at[here], dkv_ref.at[enc, core], out_recv)
    keep_out.start()
    remote(
        slots.at[other * n_enc + enc], dkv_ref.at[enc, core], out_send, out_recv, twin, enc
    ).start()

    for swap in swaps:
        swap.wait_send()

    def drain(a, carry):
        for way in range(2):
            ag_copy(way, a, 0, 1).wait_send()
            ag_copy(way, a, 0, 2).wait_send()
            ag_copy(way, a, 2, 1).wait_send()
            for kind in (0, 2, 3):
                rs_copy(way, kind, a, along[way][0]).wait_send()
        far_copy(a).wait_send()
        rs_copy(side_of(a), 1, a, along[0][0]).wait_send()
        return carry

    lax.fori_loop(0, HALF_KV, drain, 0)
    dq_keep.wait()
    dq_swap.wait()
    pltpu.make_async_copy(slots.at[pl.ds(0, tile - 1)], slots.at[pl.ds(0, tile - 1)], out_send).wait()
    pltpu.make_async_copy(dkv_ref, dkv_ref, out_recv).wait()


def finish(n_enc, dq_ref, dkv_ref, dq_out, k_out, v_out, rows, k_rows, v_rows, sem):
    half = dq_ref.shape[0] // 2
    copies = [
        pltpu.make_async_copy(dq_ref.at[pl.ds(i * half, half)], dq_out.at[pl.ds(i * half, half)], sem.at[i])
        for i in range(2)
    ]
    for copy in copies:
        copy.start()
    rows[...] = dkv_ref[...].astype(F32).reshape(rows.shape)
    for kind, (lines, out) in enumerate(((k_rows, k_out), (v_rows, v_out))):
        for h in range(KVH):
            first = h // HALF_KV * 2 * HALF_KV + kind * HALF_KV + h % HALF_KV
            lines[:, h * HD:(h + 1) * HD] = rows[pl.ds(first, n_enc, stride=4 * HALF_KV), :].astype(BF16)
        copies.append(pltpu.make_async_copy(lines, out, sem.at[2 + kind]))
        copies[-1].start()
    for copy in copies:
        copy.wait()


def shards(n_enc, queries, d_out, text_sample, tiles, img_k, img_v):
    tokens, width = queries.shape[1:]
    tile = 2 * n_enc
    span = MAX_TILES * tile
    rows = HALF_KV * 2
    vmem = pl.BlockSpec(memory_space=pltpu.VMEM)
    anywhere = pl.BlockSpec(memory_space=pl.ANY)
    dma = pltpu.SemaphoreType.DMA
    d_queries, d_own = pl.pallas_call(
        functools.partial(kernel, n_enc),
        out_shape=(
            pltpu.VMEM((tokens, width), BF16),
            pltpu.VMEM((n_enc, 2, rows, HD), BF16),
        ),
        in_specs=[anywhere] * 6,
        out_specs=(anywhere, anywhere),
        scratch_shapes=[
            pltpu.SMEM((1, SAMP), jnp.int32),
            pltpu.VMEM((2, 1, tokens), jnp.int32),
            pltpu.VMEM((2, n_enc, KVH * HD), BF16),
            pltpu.VMEM((n_enc, 2, rows, HD), BF16),
            pltpu.VMEM((2 * tokens, HD), BF16),
            pltpu.VMEM((2, tokens, width // 2), BF16),
            pltpu.VMEM((2, tokens, width // 2), BF16),
            pltpu.VMEM((2, tokens, width // 2), BF16),
            pltpu.VMEM((tile, rows, HD), BF16),
            pltpu.VMEM((tile * rows, HD), F32),
            pltpu.VMEM((RING, HALF_KV, 2, tile, HD), BF16),
            pltpu.VMEM((RATIO, span, 2 * tokens), F32),
            pltpu.VMEM((RATIO, span, 2 * tokens), F32),
            pltpu.VMEM((HALF_KV * RATIO, span, 2 * tokens), BF16),
            pltpu.VMEM((HALF_KV * RATIO, 2 * tokens, 2 * HD), BF16),
            pltpu.VMEM((HALF_KV * RATIO, 2 * tokens, 2 * HD), BF16),
            pltpu.VMEM((HALF_KV, RING, 2, tile, HD), F32),
            pltpu.VMEM((2, 4, HALF_KV, 2, tile, HD), BF16),
            pltpu.VMEM((2, 4, HALF_KV, 2, tile, HD), BF16),
            dma((2,)),
            dma((3,)),
            dma((3,)),
            dma,
            dma,
            dma((2, 4, HALF_KV)),
            dma((2, 4, HALF_KV)),
            dma((2, 4, HALF_KV)),
            dma((2, 4, HALF_KV)),
            dma,
            dma,
            dma,
            dma,
            dma,
            dma((4,)),
        ],
        compiler_params=pltpu.CompilerParams(
            collective_id=0, has_side_effects=True, vmem_limit_bytes=VMEM_LIMIT
        ),
    )(
        tiles,
        text_sample,
        img_k.reshape(n_enc, KVH * HD),
        img_v.reshape(n_enc, KVH * HD),
        queries[0],
        d_out[0],
    )
    d_queries, back_keys, back_values = pl.pallas_call(
        functools.partial(finish, n_enc),
        out_shape=(
            jax.ShapeDtypeStruct((tokens, width), BF16),
            jax.ShapeDtypeStruct((n_enc, KVH * HD), BF16),
            jax.ShapeDtypeStruct((n_enc, KVH * HD), BF16),
        ),
        in_specs=[vmem, vmem],
        out_specs=(anywhere, anywhere, anywhere),
        scratch_shapes=[
            pltpu.VMEM((n_enc * 2 * rows, HD), F32),
            pltpu.VMEM((n_enc, KVH * HD), BF16),
            pltpu.VMEM((n_enc, KVH * HD), BF16),
            dma((4,)),
        ],
        compiler_params=pltpu.CompilerParams(vmem_limit_bytes=VMEM_LIMIT // 4),
    )(d_queries, d_own)
    return (
        d_queries[None],
        back_keys.reshape(n_enc, 1, KVH * HD),
        back_values.reshape(n_enc, 1, KVH * HD),
    )


def solution(mesh):
    in_specs = (
        P("enc", "ctx", None),
        P("enc", "ctx", None),
        P("enc", "ctx"),
        P("enc", None),
        P(None, ("ctx", "enc"), None),
        P(None, ("ctx", "enc"), None),
    )
    out_specs = (
        P("enc", "ctx", None),
        P(None, ("ctx", "enc"), None),
        P(None, ("ctx", "enc"), None),
    )
    return jax.shard_map(
        functools.partial(shards, mesh.shape["enc"]),
        mesh=mesh,
        in_specs=in_specs,
        out_specs=out_specs,
        check_vma=False,
    )
```
